512 devices in a mesh: rep: 4 (over z_hi), shard: 128 (over y, z_lo, x, core).
Axes of the slice: x: 4, y: 4, z: 16 (z_hi: 4, z_lo: 4; z = z_hi * 4 + z_lo), core: 2. Of those that a mesh axis runs over, the one named last changes fastest.
Arguments:
- grad_stack: bfloat16 [4, 4, 3, 4096, 1536], P('rep', None, None, 'shard'), may hold values from -6 to 6
- master_weight: float32 [4, 3, 4096, 1536], P(None, None, 'shard', 'rep'), may hold values from -0.046875 to 0.046875
- moment_one: float32 [4, 3, 4096, 1536], P(None, None, 'shard', 'rep'), may hold values from -0.18 to 0.18
- moment_two: float32 [4, 3, 4096, 1536], P(None, None, 'shard', 'rep'), may hold values from 0.02 to 0.2
- decode_rows: bfloat16 [2560, 4096], P('shard'), may hold values from -6 to 6
- norm_gain: bfloat16 [2, 4096], replicated, may hold values from 0.5 to 1.5
- route_ids: int32 [2, 2560, 2], P(None, 'shard'), may hold values from 0 to 3, all different within a row
- route_weights: float32 [2, 2560, 2], P(None, 'shard'), may hold values from 0.2 to 1
Outputs:
- new_moment_one: float32 [4, 3, 4096, 1536], P(None, None, 'shard', 'rep')
- new_moment_two: float32 [4, 3, 4096, 1536], P(None, None, 'shard', 'rep')
- branch_out: bfloat16 [2, 2560, 4096], P(None, 'shard', 'rep')
The draws below stay inside these ranges and needn't reach their ends.
Inputs may be any that keep to these rules, and one draw needn't show every extreme that they name: `route_ids`: each row names 2 different experts, and every expert is named by some row.
All inputs are finite; a program needn't handle non-finite values.
Results may differ from the reference program's by a relative error of at most 0.029.
Values may be sent and summed in bfloat16 or wider, within the bound.
A program may use at most 64 MiB of HBM per device.

```python
import math
import jax
import jax.numpy as jnp
from jax import lax

D = 4096
F = 1536
EXPERTS = 4
TOPK = 2
ROWS = 2560
N_REP = 4


def draw_grad_stack(key, part):
    key = jax.random.fold_in(key, 11)
    common_key, replica_key = jax.random.split(key)
    common = jnp.clip(jax.random.normal(common_key, (EXPERTS, 3, D, F), jnp.float32), -3.0, 3.0)
    spread = jnp.clip(jax.random.normal(replica_key, (N_REP, EXPERTS, 3, D, F), jnp.float32), -3.0, 3.0)
    return (common[None] + spread).astype(jnp.bfloat16)


def steps_of(stream_key, extent, cuts, least, top_value):
    loudness, own = 1.0, jax.random.fold_in(stream_key, 6)
    for axis_at, parts in cuts:
        draws = jnp.exp(jax.random.uniform(jax.random.fold_in(own, axis_at), (parts,), jnp.float32, least / len(cuts), top_value / len(cuts)))
        loudness = loudness * jnp.repeat(draws, extent[axis_at] // parts).reshape([-1 if axis == axis_at else 1 for axis in range(len(extent))])
    return loudness


def different_ones(key, rows, count, top, lift):
    sequence = jax.random.permutation(jax.random.fold_in(key, 1), count)
    boost = sequence
    for power in range(3):
        boost = boost * boost // count
    boost = boost * lift // count
    lots = jax.random.randint(jax.random.fold_in(key, 2), (rows, count), 0, 4096) + boost
    fixed_rows = jax.random.permutation(jax.random.fold_in(key, 3), rows)[jnp.arange(count) % rows]
    lots = jnp.where(jnp.arange(rows)[:, None] == fixed_rows[None, :], 1 << 14, lots)
    priority = lots * count + jnp.arange(count)
    return lax.top_k(priority.astype(jnp.int32), top)[1].astype(jnp.int32)


def gaussian(own_key, dims, scale, limit, shards=(), held_as=jnp.bfloat16):
    values = scale * jax.random.normal(own_key, dims, jnp.float32)
    if shards:
        values = values * steps_of(own_key, dims, shards, -0.22, 0.18)
    return jnp.clip(values, -limit, limit).astype(held_as)


def setup_inputs(seed: int = 0) -> dict:
    key_list = jax.random.split(jax.random.key(seed), 9)
    grad_stack = draw_grad_stack(jax.random.fold_in(key_list[8], 71), 0)
    master_weight = gaussian(key_list[1], (EXPERTS, 3, D, F), (4 * D) ** -0.5, 0.046875, ((2, 128), (3, 4)), jnp.float32)
    moment_one = gaussian(key_list[2], (EXPERTS, 3, D, F), 0.03, 0.18, ((2, 128), (3, 4)), jnp.float32)
    moment_two = jnp.clip(jnp.exp(math.log(0.2) - 2.3025851 * jax.random.uniform(key_list[3], (EXPERTS, 3, D, F), jnp.float32) ** steps_of(key_list[3], (EXPERTS, 3, D, F), ((2, 128), (3, 4)), -0.2, 0.2)), 0.02, 0.2)
    decode_rows = gaussian(key_list[4], (ROWS, D), 1.0, 6.0, ((0, 128),))
    norm_gain = jnp.clip(1.0 + 0.1 * jax.random.normal(key_list[5], (2, D), jnp.float32), 0.5, 1.5).astype(jnp.bfloat16)
    route_ids = different_ones(key_list[6], 2 * ROWS, EXPERTS, TOPK, 4096).reshape((2, ROWS, TOPK))
    route_weights = jnp.clip(jnp.exp(math.log(1.0) - 1.609438 * jax.random.uniform(key_list[7], (2, ROWS, TOPK), jnp.float32) ** steps_of(key_list[7], (2, ROWS, TOPK), ((1, 128),), -0.2, 0.2)), 0.2, 1.0)
    return dict(grad_stack=grad_stack, master_weight=master_weight, moment_one=moment_one, moment_two=moment_two, decode_rows=decode_rows, norm_gain=norm_gain, route_ids=route_ids, route_weights=route_weights)


beta_one = 0.9
beta_two = 0.95
learn_rate = 0.05
adam_eps = 1e-08
bias_one = 1.0 - 0.9 ** 10
bias_two = 1.0 - 0.95 ** 10

def one_step(hidden_rows, gain_row, served, chosen_ids, chosen_weights):
    mean_sq = lax.optimization_barrier(jnp.mean(hidden_rows.astype(jnp.float32) ** 2, axis=-1, keepdims=True))
    normed = (hidden_rows.astype(jnp.float32) * lax.rsqrt(mean_sq + 1e-06) * gain_row.astype(jnp.float32)).astype(jnp.bfloat16)
    chosen = chosen_ids[:, :, None] == jnp.arange(EXPERTS, dtype=jnp.int32)[None, None, :]
    share = lax.optimization_barrier(jnp.sum(jnp.where(chosen, chosen_weights[:, :, None], 0.0), axis=1))
    weights32 = served.astype(jnp.float32)
    normed32 = normed.astype(jnp.float32)
    gate_act = jnp.einsum('rd,edf->erf', normed32, weights32[:, 0])
    up_act = jnp.einsum('rd,edf->erf', normed32, weights32[:, 1])
    hidden = (jax.nn.silu(gate_act) * up_act).astype(jnp.bfloat16)
    expert_out = jnp.einsum('erf,edf->erd', hidden.astype(jnp.float32), weights32[:, 2])
    return jnp.einsum('erd,re->rd', expert_out, share).astype(jnp.bfloat16)

def reference(grad_stack, master_weight, moment_one, moment_two, decode_rows, norm_gain, route_ids, route_weights):
    grad_mean = lax.optimization_barrier(jnp.sum(grad_stack.astype(jnp.float32), axis=0)) / N_REP
    new_one = beta_one * moment_one + (1.0 - beta_one) * grad_mean
    new_two = beta_two * moment_two + (1.0 - beta_two) * grad_mean * grad_mean
    update = new_one / bias_one / (jnp.sqrt(new_two / bias_two) + adam_eps)
    served = (master_weight - learn_rate * update).astype(jnp.bfloat16)
    first_out = one_step(decode_rows, norm_gain[0], served, route_ids[0], route_weights[0])
    middle = (decode_rows.astype(jnp.float32) + first_out.astype(jnp.float32)).astype(jnp.bfloat16)
    second_out = one_step(middle, norm_gain[1], served, route_ids[1], route_weights[1])
    return (new_one, new_two, jnp.stack([first_out, second_out]))
```

```python
import jax
import jax.numpy as jnp
from jax import lax
from jax.experimental import pallas as pl
from jax.experimental.pallas import tpu as pltpu
from jax.sharding import PartitionSpec as P

beta_one = 0.9
beta_two = 0.95
learn_rate = 0.05
adam_eps = 1e-08
bias_one = 1.0 - 0.9**10
bias_two = 1.0 - 0.95**10

MESH = pl.DeviceIdType.MESH
F32 = jnp.float32
BF16 = jnp.bfloat16

EXPERTS = 4
D = 4096
SLICE = 32
HID = 384
OWN = 20
PAD = 24
WIDE = 32
GROUP = 8
ROWS = OWN * GROUP
PADDED = PAD * GROUP
CHIP = 2 * PAD
LOCAL = 512
BATCHES = 6
SEG = 128


def div_by(value, count):
    scale = {20: 3277, 24: 2731}[count]
    return (value * scale) >> 16


def iota(shape, dim):
    return lax.broadcasted_iota(jnp.int32, shape, dim)


def one_hot(mask):
    return jnp.where(mask, 1.0, 0.0).astype(BF16)


def dot(a, b):
    return jnp.dot(a, b, preferred_element_type=F32)


def dot_last(a, b):
    return lax.dot_general(a, b, (((1,), (1,)), ((), ())), preferred_element_type=F32)


def wait_bytes(ref, sem):
    pltpu.make_async_copy(ref, ref, sem).wait()


def kernel(
    grads,
    master,
    mom1,
    mom2,
    rows,
    gain,
    ids,
    weights,
    new1,
    new2,
    out,
    W,
    RA,
    SB,
    RR,
    R32,
    XS,
    XR,
    RT,
    PA,
    PB,
    CR,
    TB,
    ZR,
    SQS,
    SQR,
    HB,
    HO,
    YB,
    YR,
    BR,
    OB,
    OR,
    sa_s,
    sa_r,
    sr_s,
    sr_r,
    ag_s,
    ag_r,
    sx_s,
    sx_r,
    st_s,
    st_r,
):
    h = lax.axis_index("rep")
    shard = lax.axis_index("shard")
    c = lax.rem(shard, 2)
    x = lax.rem(lax.div(shard, 2), 4)
    z = lax.rem(lax.div(shard, 8), 4)
    y = lax.div(shard, 32)
    t = z * 2 + c

    def at(yy, zz, xx, cc):
        return ((yy * 4 + zz) * 4 + xx) * 2 + cc

    def ahead(value, by):
        return lax.rem(value + by, 4)

    rep_peers = [(ahead(h, by), shard) for by in (1, 2, 3)]
    x_peers = [(h, at(y, z, ahead(x, by), c)) for by in (1, 2, 3)]
    y_peers = [(h, at(ahead(y, by), z, x, c)) for by in (1, 2, 3)]
    z_steps = [ahead(z, by) for by in (1, 2, 3)]
    z_peers = [(h, at(y, zz, x, c)) for zz in z_steps]
    core_peer = (h, at(y, z, x, 1 - c))
    group_steps = [(zz, c) for zz in z_steps]
    group_steps += [(zz, 1 - c) for zz in [z] + z_steps]
    group_peers = [(h, at(y, zz, x, cc)) for zz, cc in group_steps]

    def send(src, dst, s_sem, r_sem, to):
        pltpu.make_async_remote_copy(
            src_ref=src,
            dst_ref=dst,
            send_sem=s_sem,
            recv_sem=r_sem,
            device_id=to,
            device_id_type=MESH,
        ).start()

    barrier = pltpu.get_barrier_semaphore()
    everyone = rep_peers + x_peers + y_peers + group_peers
    for peer in everyone:
        pl.semaphore_signal(barrier, inc=1, device_id=peer, device_id_type=MESH)

    R32[...] = jnp.zeros(R32.shape, BF16)
    R32[0:OWN, :] = rows[...]
    q = iota((256, 256), 1)
    r = iota((256, 256), 0)
    q_src = ((q & 127) >> 5) * 64 + (q >> 7) * 32 + (q & 31)
    r_src = ((r & 127) >> 5) * 64 + (r >> 7) * 32 + (r & 31)
    perm = one_hot(r == q_src)
    perm_back = one_hot(q == r_src)
    for zz in range(4):
        for yy in range(4):
            first = yy * 1024 + zz * 256
            moved = dot(R32[:, first : first + 256], perm).astype(BF16)
            XS[2 * zz, :, yy * SEG : (yy + 1) * SEG] = moved[:, 0:SEG]
            XS[2 * zz + 1, :, yy * SEG : (yy + 1) * SEG] = moved[:, SEG : 2 * SEG]
    XR[t] = XS[t]
    lane = iota((OWN, 128), 1)
    tile = jnp.zeros((OWN, 128), F32)
    for s in range(2):
        for k in range(2):
            tile = jnp.where(lane == 4 * s + 2 * k, ids[s, :, k : k + 1].astype(F32), tile)
            tile = jnp.where(lane == 4 * s + 2 * k + 1, weights[s, :, k : k + 1], tile)
    RT[t] = jnp.zeros((PAD, 128), F32)
    RT[t, 0:OWN, :] = tile

    def pick(n_to, n_from, to_len, from_len):
        a, b = iota((n_to, n_from), 0), iota((n_to, n_from), 1)
        ta = a >> 5 if to_len == 32 else div_by(a, to_len)
        tb = b >> 5 if from_len == 32 else div_by(b, from_len)
        ia, ib = a - ta * to_len, b - tb * from_len
        return one_hot((ta == tb) & (ia == ib) & (ia < OWN))

    gains = []
    for s in range(2):
        parts = []
        for yy in range(4):
            first = pl.multiple_of(yy * 1024 + z * 256, 256)
            both = dot(gain[:, pl.ds(first, 256)], perm)
            parts.append(jnp.where(c == 0, both[s : s + 1, 0:SEG], both[s : s + 1, SEG : 2 * SEG]))
        gains.append(jnp.concatenate(parts, axis=1))

    pl.semaphore_wait(barrier, len(everyone))

    hp, hm, h2 = ahead(h, 1), ahead(h, 3), ahead(h, 2)
    up_peer, down_peer = (hp, shard), (hm, shard)

    def columns(owner):
        return pl.ds(pl.multiple_of(owner * HID, HID), HID)

    def pieces(b):
        if b < 4:
            return (b, slice(0, 2))
        return (slice(2 * (b - 4), 2 * (b - 4) + 2), 2)

    def grad_at(b, first, last, owner):
        return (0, *pieces(b), slice(first, last), columns(owner))

    def send_across(b):
        send(grads.at[grad_at(b, 0, 16, h2)], RA.at[b, 0], sa_s.at[b, 0], sa_r.at[b, 0], up_peer)
        send(grads.at[grad_at(b, 16, 32, h2)], RA.at[b, 1], sa_s.at[b, 1], sa_r.at[b, 1], down_peer)

    def send_plain(b):
        send(grads.at[grad_at(b, 16, 32, hp)], RR.at[b, 0, :, 16:32], sr_s.at[b, 0], sr_r.at[b, 0], up_peer)
        send(grads.at[grad_at(b, 0, 16, hm)], RR.at[b, 1, :, 0:16], sr_s.at[b, 1], sr_r.at[b, 1], down_peer)

    def send_summed(b):
        wait_bytes(RA.at[b, 0], sa_r.at[b, 0])
        SB[b, 0] = (RA[b, 0].astype(F32) + grads[grad_at(b, 0, 16, hp)].astype(F32)).astype(BF16)
        send(SB.at[b, 0], RR.at[b, 0, :, 0:16], sr_s.at[b, 0], sr_r.at[b, 0], up_peer)
        wait_bytes(RA.at[b, 1], sa_r.at[b, 1])
        SB[b, 1] = (RA[b, 1].astype(F32) + grads[grad_at(b, 16, 32, hm)].astype(F32)).astype(BF16)
        send(SB.at[b, 1], RR.at[b, 1, :, 16:32], sr_s.at[b, 1], sr_r.at[b, 1], down_peer)

    def refit(b):
        wait_bytes(RR.at[b, 0], sr_r.at[b, 0])
        wait_bytes(RR.at[b, 1], sr_r.at[b, 1])
        total = grads[grad_at(b, 0, 32, h)].astype(F32) + RR[b, 0].astype(F32) + RR[b, 1].astype(F32)
        mean = total * 0.25
        where = pieces(b)
        one = beta_one * mom1[where] + (1.0 - beta_one) * mean
        two = beta_two * mom2[where] + (1.0 - beta_two) * mean * mean
        new1[where] = one
        new2[where] = two
        update = one / bias_one / (jnp.sqrt(two / bias_two) + adam_eps)
        W[b, :, y, x] = (master[where] - learn_rate * update).astype(BF16)
        for peer in x_peers:
            send(W.at[b, 0, y, x], W.at[b, 0, y, x], ag_s.at[b, 0, 0], ag_r.at[b, 0, 0], peer)
        for peer in y_peers:
            send(W.at[b, 1, y, x], W.at[b, 1, y, x], ag_s.at[b, 0, 1], ag_r.at[b, 0, 1], peer)

    def pass_on(b):
        wait_bytes(W.at[b, 0, 0, 0:3], ag_r.at[b, 0, 0])
        for peer in y_peers:
            send(W.at[b, 0, y], W.at[b, 0, y], ag_s.at[b, 1, 0], ag_r.at[b, 1, 0], peer)
        wait_bytes(W.at[b, 1, 0, 0:3], ag_r.at[b, 0, 1])
        for peer in x_peers:
            send(W.at[b, 1, :, x], W.at[b, 1, :, x], ag_s.at[b, 1, 1], ag_r.at[b, 1, 1], peer)

    def gathered(b):
        wait_bytes(W.at[b, 0, 0:3], ag_r.at[b, 1, 0])
        wait_bytes(W.at[b, 1, 0:3], ag_r.at[b, 1, 1])

    def rows_in():
        wait_bytes(XR.at[0:7], sx_r.at[0, 0])
        wait_bytes(RT.at[0:7], st_r.at[0])

    def route_column(s, k):
        return RT[...].reshape(PADDED, 128)[:, 4 * s + 2 * k : 4 * s + 2 * k + 1]

    def send_squares(s, raw):
        squares = jnp.sum(raw * raw, axis=1, keepdims=True)
        same = iota((CHIP, 128), 0) == iota((CHIP, 128), 1)
        for zz in range(4):
            part = squares[zz * CHIP : (zz + 1) * CHIP]
            line = jnp.sum(jnp.where(same, part, 0.0), axis=0, keepdims=True)
            SQS[s, zz] = jnp.broadcast_to(line, (8, 128))
        SQR[s, t] = SQS[s, z]
        for (zz, _), peer in zip(group_steps, group_peers):
            send(SQS.at[s, zz], SQR.at[s, t], st_s.at[1 + s], st_r.at[1 + s], peer)

    def first_product(s, e, activations, choice):
        gate = dot(activations, W[e, 0].reshape(LOCAL, HID))
        up = dot(activations, W[e, 1].reshape(LOCAL, HID))
        for k in range(2):
            chosen = choice[k] == float(e)
            PA[k, 0] = PA[k, 0] + jnp.where(chosen, gate, 0.0)
            PA[k, 1] = PA[k, 1] + jnp.where(chosen, up, 0.0)

    def swap_cores(s):
        PB[s] = PA[...].astype(BF16)
        send(PB.at[s, 1 - c], CR.at[s], sx_s.at[1, s], sx_r.at[1, s], core_peer)

    def sum_group(s):
        wait_bytes(CR.at[s], sx_r.at[1, s])
        for g in range(2):
            both = PB[s, c, g].astype(F32) + CR[s, g].astype(F32)
            for zz in range(4):
                TB[s, zz, g] = both[zz * CHIP : (zz + 1) * CHIP].astype(BF16)
        for zz, peer in zip(z_steps, z_peers):
            send(TB.at[s, zz], ZR.at[s, z], sx_s.at[2, s], sx_r.at[2, s], peer)
        ZR[s, z] = TB[s, z]

    def hidden_units(s):
        wait_bytes(SQR.at[s, 0:7], st_r.at[1 + s])
        total = jnp.sum(SQR[s][:, 0, :], axis=0, keepdims=True)
        scale_line = lax.rsqrt(total / float(D) + 1e-06)
        same = iota((CHIP, 128), 0) == iota((CHIP, 128), 1)
        scale = jnp.sum(jnp.where(same, scale_line, 0.0), axis=1, keepdims=True)
        routes = RT[pl.ds(2 * z, 2)].reshape(CHIP, 128)
        share = jnp.where(c == 0, routes[:, 4 * s + 1 : 4 * s + 2], routes[:, 4 * s + 3 : 4 * s + 4])
        wait_bytes(ZR.at[s, 0:3], sx_r.at[2, s])
        parts = [ZR[s, zz].astype(F32) for zz in range(4)]
        both = (parts[0] + parts[1]) + (parts[2] + parts[3])
        gate, up = both[0] * scale, both[1] * scale
        HB[s, z] = (jax.nn.silu(gate) * up * share).astype(BF16)
        for peer in z_peers:
            send(HB.at[s, z], HB.at[s, z], sx_s.at[3, s], sx_r.at[3, s], peer)

    def swap_hidden(s):
        wait_bytes(HB.at[s, 0:3], sx_r.at[3, s])
        send(HB.at[s], HO.at[s], sx_s.at[4, s], sx_r.at[4, s], core_peer)

    def second_product(packed, choice, total):
        for e in range(EXPERTS):
            mine = jnp.where(choice == float(e), packed, 0.0).astype(BF16)
            part = dot_last(mine, W[4 + e // 2, e % 2].reshape(LOCAL, HID))
            total = part if total is None else total + part
        return total

    def send_sums(s, total):
        for hh in range(4):
            YB[s, hh] = total[:, hh * SEG : (hh + 1) * SEG].astype(BF16)
        for peer in rep_peers:
            send(YB.at[s, peer[0]], YR.at[s, h], sx_s.at[5, s], sx_r.at[5, s], peer)
        YR[s, h] = YB[s, h]

    def branch_part(s):
        wait_bytes(YR.at[s, 0:3], sx_r.at[5, s])
        parts = [YR[s, hh].astype(F32) for hh in range(4)]
        return ((parts[0] + parts[1]) + (parts[2] + parts[3])).astype(BF16)

    def send_home(s, part, spread):
        OB[s] = dot(spread, part).astype(BF16).reshape(GROUP, WIDE, SEG)
        OR[s, t] = OB[s, t]
        for (zz, cc), peer in zip(group_steps, group_peers):
            send(OB.at[s, 2 * zz + cc], OR.at[s, t], sx_s.at[6, s], sx_r.at[6, s], peer)

    def store_home(s):
        wait_bytes(OR.at[s, 0:7], sx_r.at[6, s])
        for zz in range(4):
            both = jnp.concatenate([OR[s, 2 * zz], OR[s, 2 * zz + 1]], axis=1)
            out[s, :, zz * 256 : (zz + 1) * 256] = dot(both, perm_back).astype(BF16)[0:OWN]

    send_across(0)
    send_plain(0)
    send_across(1)
    for (zz, cc), peer in zip(group_steps, group_peers):
        send(XS.at[2 * zz + cc], XR.at[t], sx_s.at[0, 0], sx_r.at[0, 0], peer)
        send(RT.at[t], RT.at[t], st_s.at[0], st_r.at[0], peer)

    def first_rows():
        rows_in()
        arrived = XR[...].reshape(GROUP * WIDE, LOCAL)
        raw_packed = dot(pick(ROWS, GROUP * WIDE, OWN, WIDE), arrived)
        raw = dot(pick(PADDED, GROUP * WIDE, PAD, WIDE), arrived)
        return raw_packed, raw

    for b in range(BATCHES + 1):
        if b < BATCHES:
            send_summed(b)
            if b + 1 < BATCHES:
                send_plain(b + 1)
            if b + 2 < BATCHES:
                send_across(b + 2)
        if b >= 1:
            refit(b - 1)
        if b >= 2:
            pass_on(b - 2)
        if b == 2:
            raw_packed, raw = first_rows()
            send_squares(0, raw)
            acts = (raw * gains[0]).astype(BF16)
            choice = [route_column(0, k) for k in range(2)]
            PA[...] = jnp.zeros(PA.shape, F32)
        if 3 <= b < 3 + EXPERTS:
            gathered(b - 3)
            first_product(0, b - 3, acts, choice)

    pack = pick(ROWS, PADDED, OWN, PAD)
    unpack = pick(PADDED, ROWS, PAD, OWN)
    spread = pick(GROUP * WIDE, ROWS, WIDE, OWN)
    routes_packed = dot(pack, RT[...].reshape(PADDED, 128).astype(BF16))

    def packed_choice(s, k):
        return routes_packed[:, 4 * s + 2 * k : 4 * s + 2 * k + 1]

    def rest_of_step(s):
        own_choice = jnp.where(c == 0, packed_choice(s, 0), packed_choice(s, 1))
        other_choice = jnp.where(c == 0, packed_choice(s, 1), packed_choice(s, 0))
        swap_hidden(s)
        total = second_product(dot(pack, HB[s].reshape(PADDED, HID)), own_choice, None)
        wait_bytes(HO.at[s], sx_r.at[4, s])
        total = second_product(dot(pack, HO[s].reshape(PADDED, HID)), other_choice, total)
        send_sums(s, total)
        return branch_part(s)

    swap_cores(0)
    pass_on(BATCHES - 1)
    sum_group(0)
    hidden_units(0)
    gathered(4)
    gathered(5)
    part = rest_of_step(0)

    BR[h] = part
    for peer in rep_peers:
        send(BR.at[h], BR.at[h], sx_s.at[0, 1], sx_r.at[0, 1], peer)
    send_home(0, part, spread)
    wait_bytes(BR.at[0:3], sx_r.at[0, 1])
    branch = jnp.concatenate([BR[hh] for hh in range(4)], axis=1).astype(F32)
    middle = (raw_packed + branch).astype(BF16)
    raw = dot(unpack, middle)
    send_squares(1, raw)
    acts = (raw * gains[1]).astype(BF16)
    choice = [route_column(1, k) for k in range(2)]
    PA[...] = jnp.zeros(PA.shape, F32)
    for e in range(EXPERTS):
        first_product(1, e, acts, choice)
    swap_cores(1)
    sum_group(1)
    hidden_units(1)
    part = rest_of_step(1)
    send_home(1, part, spread)
    store_home(0)
    store_home(1)

    for b in range(BATCHES):
        for way in range(2):
            wait_bytes(RA.at[b, way], sa_s.at[b, way])
            wait_bytes(RR.at[b, way], sr_s.at[b, way])
        for p in range(2):
            wait_bytes(W.at[b, p, 0, 0:3], ag_s.at[b, 0, p])
            wait_bytes(W.at[b, p, 0:3], ag_s.at[b, 1, p])
    wait_bytes(XS.at[0:7], sx_s.at[0, 0])
    wait_bytes(RT.at[0:7], st_s.at[0])
    wait_bytes(BR.at[0:3], sx_s.at[0, 1])
    for s in range(2):
        wait_bytes(SQR.at[s, 0:7], st_s.at[1 + s])
        wait_bytes(CR.at[s], sx_s.at[1, s])
        wait_bytes(ZR.at[s, 0:3], sx_s.at[2, s])
        wait_bytes(HB.at[s, 0:3], sx_s.at[3, s])
        wait_bytes(HO.at[s], sx_s.at[4, s])
        wait_bytes(YR.at[s, 0:3], sx_s.at[5, s])
        wait_bytes(OR.at[s, 0:7], sx_s.at[6, s])


def shards(grad_stack, master_weight, moment_one, moment_two, decode_rows, norm_gain, route_ids, route_weights):
    dma = pltpu.SemaphoreType.DMA
    vmem = pltpu.VMEM
    scratch = [
        vmem((BATCHES, 2, 4, 4, SLICE, HID), BF16),
        vmem((BATCHES, 2, 2, 16, HID), BF16),
        vmem((BATCHES, 2, 2, 16, HID), BF16),
        vmem((BATCHES, 2, 2, SLICE, HID), BF16),
        vmem((WIDE, D), BF16),
        vmem((GROUP, WIDE, LOCAL), BF16),
        vmem((GROUP, WIDE, LOCAL), BF16),
        vmem((GROUP, PAD, 128), F32),
        vmem((2, 2, PADDED, HID), F32),
        vmem((2, 2, 2, PADDED, HID), BF16),
        vmem((2, 2, PADDED, HID), BF16),
        vmem((2, 4, 2, CHIP, HID), BF16),
        vmem((2, 4, 2, CHIP, HID), BF16),
        vmem((2, 4, 8, 128), F32),
        vmem((2, GROUP, 8, 128), F32),
        vmem((2, 4, CHIP, HID), BF16),
        vmem((2, 4, CHIP, HID), BF16),
        vmem((2, 4, ROWS, SEG), BF16),
        vmem((2, 4, ROWS, SEG), BF16),
        vmem((4, ROWS, SEG), BF16),
        vmem((2, GROUP, WIDE, SEG), BF16),
        vmem((2, GROUP, WIDE, SEG), BF16),
        dma((BATCHES, 2)),
        dma((BATCHES, 2)),
        dma((BATCHES, 2)),
        dma((BATCHES, 2)),
        dma((BATCHES, 2, 2)),
        dma((BATCHES, 2, 2)),
        dma((7, 2)),
        dma((7, 2)),
        dma((3,)),
        dma((3,)),
    ]
    in_vmem = pl.BlockSpec(memory_space=pltpu.VMEM)
    return pl.pallas_call(
        kernel,
        out_shape=(
            jax.ShapeDtypeStruct(moment_one.shape, F32),
            jax.ShapeDtypeStruct(moment_two.shape, F32),
            jax.ShapeDtypeStruct((2, OWN, D // 4), BF16),
        ),
        in_specs=[in_vmem] * 8,
        out_specs=(in_vmem,) * 3,
        scratch_shapes=scratch,
        compiler_params=pltpu.CompilerParams(
            collective_id=0, has_side_effects=True, vmem_limit_bytes=40 * 1024 * 1024
        ),
        name="refit_and_decode",
    )(grad_stack, master_weight, moment_one, moment_two, decode_rows, norm_gain, route_ids, route_weights)


def solution(mesh):
    return jax.shard_map(
        shards,
        mesh=mesh,
        in_specs=(
            P("rep", None, None, "shard", None),
            P(None, None, "shard", "rep"),
            P(None, None, "shard", "rep"),
            P(None, None, "shard", "rep"),
            P("shard", None),
            P(),
            P(None, "shard", None),
            P(None, "shard", None),
        ),
        out_specs=(
            P(None, None, "shard", "rep"),
            P(None, None, "shard", "rep"),
            P(None, "shard", "rep"),
        ),
        check_vma=False,
    )
```

```python
import jax
import jax.numpy as jnp
from jax import lax
from jax.experimental import pallas as pl
from jax.experimental.pallas import tpu as pltpu
from jax.sharding import PartitionSpec as P

beta_one = 0.9
beta_two = 0.95
learn_rate = 0.05
adam_eps = 1e-08
bias_one = 1.0 - 0.9**10
bias_two = 1.0 - 0.95**10

MESH = pl.DeviceIdType.MESH
F32 = jnp.float32
BF16 = jnp.bfloat16

EXPERTS = 4
D = 4096
SLICE = 32
HID = 384
OWN = 20
PAD = 24
WIDE = 32
GROUP = 8
ROWS = OWN * GROUP
PADDED = PAD * GROUP
HALF = PADDED // 2
HALF_ROWS = ROWS // 2
BOTH = 2 * PAD
PACKED = 80
LOCAL = 512
BATCHES = 6
SEG = 128


def div_by(value, count):
    scale = {20: 3277, 24: 2731}[count]
    return (value * scale) >> 16


def iota(shape, dim):
    return lax.broadcasted_iota(jnp.int32, shape, dim)


def one_hot(mask):
    return jnp.where(mask, 1.0, 0.0).astype(BF16)


def dot(a, b):
    return jnp.dot(a, b, preferred_element_type=F32)


def dot_last(a, b):
    return lax.dot_general(a, b, (((1,), (1,)), ((), ())), preferred_element_type=F32)


def wait_bytes(ref, sem):
    pltpu.make_async_copy(ref, ref, sem).wait()


def kernel(
    grads,
    master,
    mom1,
    mom2,
    rows,
    gain,
    ids,
    weights,
    new1,
    new2,
    out,
    GV,
    MV,
    N1,
    N2,
    W,
    RA,
    SB,
    RR,
    RV,
    GN,
    IV,
    WV,
    R32,
    XS,
    XR,
    RT,
    PA,
    PB,
    CR,
    TB,
    ZR,
    SQS,
    SQR,
    HB,
    HO,
    YB,
    YR,
    BR,
    OB,
    OR,
    in_sem,
    out_sem,
    sa_s,
    sa_r,
    sr_s,
    sr_r,
    ag_s,
    ag_r,
    sx_s,
    sx_r,
    st_s,
    st_r,
):
    h = lax.axis_index("rep")
    shard = lax.axis_index("shard")
    c = lax.rem(shard, 2)
    x = lax.rem(lax.div(shard, 2), 4)
    z = lax.rem(lax.div(shard, 8), 4)
    y = lax.div(shard, 32)
    t = c * 4 + z

    def at(yy, zz, xx, cc):
        return ((yy * 4 + zz) * 4 + xx) * 2 + cc

    def ahead(value, by):
        return lax.rem(value + by, 4)

    rep_peers = [(ahead(h, by), shard) for by in (1, 2, 3)]
    x_peers = [(h, at(y, z, ahead(x, by), c)) for by in (1, 2, 3)]
    y_peers = [(h, at(ahead(y, by), z, x, c)) for by in (1, 2, 3)]
    z_steps = [ahead(z, by) for by in (1, 2, 3)]
    z_peers = [(h, at(y, zz, x, c)) for zz in z_steps]
    core_peer = (h, at(y, z, x, 1 - c))
    group_steps = [(zz, c) for zz in z_steps]
    group_steps += [(zz, 1 - c) for zz in [z] + z_steps]
    group_peers = [(h, at(y, zz, x, cc)) for zz, cc in group_steps]

    place = 4 * h + z

    def near(by, cc):
        there = lax.rem(place + by + 16, 16)
        return (lax.div(there, 4), at(y, lax.rem(there, 4), x, cc))

    two = jnp.where(lax.rem(place, 2) == 0, 2, -2)
    near_steps = [(by, cc) for by in (1, -1, two) for cc in (0, 1)]

    def send(src, dst, s_sem, r_sem, to):
        pltpu.make_async_remote_copy(
            src_ref=src,
            dst_ref=dst,
            send_sem=s_sem,
            recv_sem=r_sem,
            device_id=to,
            device_id_type=MESH,
        ).start()

    barrier = pltpu.get_barrier_semaphore()
    everyone = rep_peers + x_peers + y_peers + group_peers
    everyone += [near(by, cc) for by in (1, -1, 2, -2) for cc in (0, 1)]
    for peer in everyone:
        pl.semaphore_signal(barrier, inc=1, device_id=peer, device_id_type=MESH)
    incoming = [
        pltpu.make_async_copy(grads.at[0], GV, in_sem.at[0]),
        pltpu.make_async_copy(rows, RV, in_sem.at[1]),
        pltpu.make_async_copy(gain, GN, in_sem.at[2]),
        pltpu.make_async_copy(ids, IV, in_sem.at[3]),
        pltpu.make_async_copy(master, MV.at[0], in_sem.at[4]),
        pltpu.make_async_copy(mom1, MV.at[1], in_sem.at[5]),
        pltpu.make_async_copy(mom2, MV.at[2], in_sem.at[6]),
        pltpu.make_async_copy(weights, WV, in_sem.at[7]),
    ]
    for copy in incoming:
        copy.start()

    def pick(n_to, n_from, to_len, from_len):
        a, b = iota((n_to, n_from), 0), iota((n_to, n_from), 1)
        ta = a >> 5 if to_len == 32 else div_by(a, to_len)
        tb = b >> 5 if from_len == 32 else div_by(b, from_len)
        ia, ib = a - ta * to_len, b - tb * from_len
        return one_hot((ta == tb) & (ia == ib) & (ia < OWN))

    hp, hm, h2 = ahead(h, 1), ahead(h, 3), ahead(h, 2)
    up_peer, down_peer = (hp, shard), (hm, shard)

    def columns(owner):
        return pl.ds(pl.multiple_of(owner * HID, HID), HID)

    def pieces(b):
        if b < 4:
            return (b, slice(0, 2))
        return (slice(2 * (b - 4), 2 * (b - 4) + 2), 2)

    def grad_at(b, first, last, owner):
        return (*pieces(b), slice(first, last), columns(owner))

    def send_across(b):
        send(GV.at[grad_at(b, 0, 16, h2)], RA.at[b, 0], sa_s.at[b, 0], sa_r.at[b, 0], up_peer)
        send(GV.at[grad_at(b, 16, 32, h2)], RA.at[b, 1], sa_s.at[b, 1], sa_r.at[b, 1], down_peer)

    def send_plain(b):
        src = GV.at[grad_at(b, 16, 32, hp)]
        send(src, RR.at[b, 0, :, 16:32], sr_s.at[b, 0], sr_r.at[b, 0], up_peer)
        src = GV.at[grad_at(b, 0, 16, hm)]
        send(src, RR.at[b, 1, :, 0:16], sr_s.at[b, 1], sr_r.at[b, 1], down_peer)

    def send_summed(b):
        wait_bytes(RA.at[b, 0], sa_r.at[b, 0])
        SB[b, 0] = (RA[b, 0].astype(F32) + GV[grad_at(b, 0, 16, hp)].astype(F32)).astype(BF16)
        send(SB.at[b, 0], RR.at[b, 0, :, 0:16], sr_s.at[b, 0], sr_r.at[b, 0], up_peer)
        wait_bytes(RA.at[b, 1], sa_r.at[b, 1])
        SB[b, 1] = (RA[b, 1].astype(F32) + GV[grad_at(b, 16, 32, hm)].astype(F32)).astype(BF16)
        send(SB.at[b, 1], RR.at[b, 1, :, 16:32], sr_s.at[b, 1], sr_r.at[b, 1], down_peer)

    def refit(b):
        wait_bytes(RR.at[b, 0], sr_r.at[b, 0])
        wait_bytes(RR.at[b, 1], sr_r.at[b, 1])
        total = GV[grad_at(b, 0, 32, h)].astype(F32) + RR[b, 0].astype(F32) + RR[b, 1].astype(F32)
        mean = total * 0.25
        where = pieces(b)
        one = beta_one * MV[(1, *where)] + (1.0 - beta_one) * mean
        two = beta_two * MV[(2, *where)] + (1.0 - beta_two) * mean * mean
        update = one / bias_one / (jnp.sqrt(two / bias_two) + adam_eps)
        W[b, :, y, x] = (MV[(0, *where)] - learn_rate * update).astype(BF16)
        for peer in x_peers:
            send(W.at[b, 0, y, x], W.at[b, 0, y, x], ag_s.at[b, 0, 0], ag_r.at[b, 0, 0], peer)
        for peer in y_peers:
            send(W.at[b, 1, y, x], W.at[b, 1, y, x], ag_s.at[b, 0, 1], ag_r.at[b, 0, 1], peer)
        N1[where] = one
        N2[where] = two
        pltpu.make_async_copy(N1.at[where], new1.at[where], out_sem.at[b, 0]).start()
        pltpu.make_async_copy(N2.at[where], new2.at[where], out_sem.at[b, 1]).start()

    def pass_on(b):
        wait_bytes(W.at[b, 0, 0, 0:3], ag_r.at[b, 0, 0])
        for peer in y_peers:
            send(W.at[b, 0, y], W.at[b, 0, y], ag_s.at[b, 1, 0], ag_r.at[b, 1, 0], peer)
        wait_bytes(W.at[b, 1, 0, 0:3], ag_r.at[b, 0, 1])
        for peer in x_peers:
            send(W.at[b, 1, :, x], W.at[b, 1, :, x], ag_s.at[b, 1, 1], ag_r.at[b, 1, 1], peer)

    def gathered(b):
        wait_bytes(W.at[b, 0, 0:3], ag_r.at[b, 1, 0])
        wait_bytes(W.at[b, 1, 0:3], ag_r.at[b, 1, 1])

    def permutations():
        q = iota((256, 256), 1)
        r = iota((256, 256), 0)
        q_src = ((q & 127) >> 5) * 64 + (q >> 7) * 32 + (q & 31)
        r_src = ((r & 127) >> 5) * 64 + (r >> 7) * 32 + (r & 31)
        return one_hot(r == q_src), one_hot(q == r_src)

    def cut_rows():
        R32[...] = jnp.zeros(R32.shape, BF16)
        perm = permutations()[0]
        incoming[3].wait()
        incoming[7].wait()
        diagonal = iota((PAD, OWN), 0) == iota((PAD, OWN), 1)
        lane = iota((PAD, 128), 1)
        tile = jnp.zeros((PAD, 128), F32)
        for s in range(2):
            for k in range(2):
                for first, line in ((0, IV[s, k : k + 1].astype(F32)), (4, WV[s, k : k + 1])):
                    column = jnp.sum(jnp.where(diagonal, line, 0.0), axis=1, keepdims=True)
                    tile = jnp.where(lane == first + 2 * s + k, column, tile)
        RT[t] = tile
        incoming[1].wait()
        R32[0:OWN, :] = RV[...]
        blocks = [R32[:, (4 * yy + zz) * 256 : (4 * yy + zz + 1) * 256] for zz in range(4) for yy in range(4)]
        moved = dot(jnp.concatenate(blocks, axis=0), perm).astype(BF16)
        moved = dot(pick(16 * OWN, 16 * WIDE, OWN, WIDE), moved).astype(BF16)
        for zz in range(4):
            XS[zz] = moved[4 * zz * OWN : 4 * (zz + 1) * OWN, 0:SEG]
            XS[4 + zz] = moved[4 * zz * OWN : 4 * (zz + 1) * OWN, SEG : 2 * SEG]
        XR[t] = XS[t]

    def send_rows():
        for by, cc in near_steps:
            zz = lax.rem(place + by + 16, 4)
            send(XS.at[4 * cc + zz], XR.at[t], sx_s.at[0, 0], sx_r.at[0, 0], near(by, cc))
            send(RT.at[t], RT.at[t], st_s.at[0], st_r.at[0], near(by, cc))
        send(XS.at[4 * (1 - c) + z], XR.at[t], sx_s.at[0, 0], sx_r.at[0, 0], core_peer)
        send(RT.at[t], RT.at[t], st_s.at[0], st_r.at[0], core_peer)

    def local_gains():
        incoming[2].wait()
        perm = permutations()[0]
        gains = [[], []]
        for yy in range(4):
            first = pl.multiple_of(yy * 1024 + z * 256, 256)
            both = dot(GN[:, pl.ds(first, 256)], perm)
            both = jnp.where(c == 0, both[:, 0:SEG], both[:, SEG : 2 * SEG])
            for s in range(2):
                gains[s].append(both[s : s + 1])
        return [jnp.concatenate(parts, axis=1) for parts in gains]

    def first_rows():
        wait_bytes(XR.at[0:7], sx_r.at[0, 0])
        wait_bytes(RT.at[0:7], st_r.at[0])
        a, b = iota((4 * ROWS, 4 * ROWS), 0), iota((4 * ROWS, 4 * ROWS), 1)
        to_y = sum(jnp.where(a >= n * ROWS, 1, 0) for n in (1, 2, 3))
        to_t = div_by(a - to_y * ROWS, OWN)
        source = to_t * (4 * OWN) + to_y * OWN + (a - to_y * ROWS - to_t * OWN)
        arrived = dot(one_hot(b == source), XR[...].reshape(4 * ROWS, SEG))
        raw_packed = jnp.concatenate([arrived[n * ROWS : (n + 1) * ROWS] for n in range(4)], axis=1)
        raw = dot(pick(PADDED, ROWS, PAD, OWN), raw_packed.astype(BF16))
        return raw_packed, raw

    def route_column(s, k):
        return RT[...].reshape(PADDED, 128)[:, 2 * s + k : 2 * s + k + 1]

    same = iota((PAD, 128), 0) == iota((PAD, 128), 1)

    def send_squares(s, half, raw):
        squares = jnp.sum(raw * raw, axis=1, keepdims=True)
        for zz in range(4):
            part = squares[zz * PAD : (zz + 1) * PAD]
            line = jnp.sum(jnp.where(same, part, 0.0), axis=0, keepdims=True)
            SQS[s, half, zz] = jnp.broadcast_to(line, (8, 128))
        SQR[s, half, t] = SQS[s, half, z]
        for (zz, _), peer in zip(group_steps, group_peers):
            src = SQS.at[s, half, zz]
            send(src, SQR.at[s, half, t], st_s.at[1 + 2 * s + half], st_r.at[1 + 2 * s + half], peer)

    def first_product(e, activations, choice, first, count):
        gate = dot(activations, W[e, 0].reshape(LOCAL, HID))
        up = dot(activations, W[e, 1].reshape(LOCAL, HID))
        for k in range(2):
            chosen = choice[k] == float(e)
            for g, value in enumerate((gate, up)):
                value = jnp.where(chosen, value, 0.0)
                if e > 0:
                    value = PA[k, g, first : first + count] + value
                PA[k, g, first : first + count] = value

    def swap_cores(s, half):
        for k in range(2):
            for g in range(2):
                PB[s, half, k, g] = PA[k, g, half * HALF : (half + 1) * HALF].astype(BF16)
        send(PB.at[s, half, 1 - c], CR.at[s, half], sx_s.at[1 + half, s], sx_r.at[1 + half, s], core_peer)

    def sum_group(s, half):
        wait_bytes(CR.at[s, half], sx_r.at[1 + half, s])
        gate = PB[s, half, c, 0].astype(F32) + CR[s, half, 0].astype(F32)
        up = PB[s, half, c, 1].astype(F32) + CR[s, half, 1].astype(F32)
        for zz in range(4):
            cut = slice(zz * PAD, (zz + 1) * PAD)
            TB[s, half, zz] = jnp.concatenate([gate[cut], up[cut]], axis=0).astype(BF16)
        for zz, peer in zip(z_steps, z_peers):
            send(TB.at[s, half, zz], ZR.at[s, half, z], sx_s.at[3 + half, s], sx_r.at[3 + half, s], peer)
        ZR[s, half, z] = TB[s, half, z]

    def hidden_units(s, half):
        wait_bytes(SQR.at[s, half, 0:7], st_r.at[1 + 2 * s + half])
        total = jnp.sum(SQR[s, half][:, 0, :], axis=0, keepdims=True)
        scale_line = lax.rsqrt(total / float(D) + 1e-06)
        scale = jnp.sum(jnp.where(same, scale_line, 0.0), axis=1, keepdims=True)
        routes = RT[4 * half + z]
        share = jnp.where(c == 0, routes[:, 4 + 2 * s : 5 + 2 * s], routes[:, 5 + 2 * s : 6 + 2 * s])
        wait_bytes(ZR.at[s, half, 0:3], sx_r.at[3 + half, s])
        parts = [ZR[s, half, zz].astype(F32) for zz in range(4)]
        both = (parts[0] + parts[1]) + (parts[2] + parts[3])
        gate, up = both[0:PAD] * scale, both[PAD:BOTH] * scale
        units = jax.nn.silu(gate) * up * share
        blocks = [units[:, i * 128 : (i + 1) * 128] for i in range(3)]
        blocks.append(jnp.zeros((PACKED - 3 * PAD, 128), F32))
        HB[s, half, z] = jnp.concatenate(blocks, axis=0).astype(BF16)
        for peer in z_peers:
            send(HB.at[s, half, z], HB.at[s, half, z], sx_s.at[5 + half, s], sx_r.at[5 + half, s], peer)

    def swap_hidden(s, half):
        wait_bytes(HB.at[s, half, 0:3], sx_r.at[5 + half, s])
        send(HB.at[s, half], HO.at[s, half], sx_s.at[7 + half, s], sx_r.at[7 + half, s], core_peer)

    def second_product(units, choice, total):
        flat = dot(pack, units.reshape(4 * PACKED, 128))
        flat = jnp.concatenate([flat[i * HALF_ROWS : (i + 1) * HALF_ROWS] for i in range(3)], axis=1)
        for e in range(EXPERTS):
            mine = jnp.where(choice == float(e), flat, 0.0).astype(BF16)
            part = dot_last(mine, W[4 + e // 2, e % 2].reshape(LOCAL, HID))
            total = part if total is None else total + part
        return total

    def send_sums(s, half, total):
        for hh in range(4):
            YB[s, half, hh] = total[:, hh * SEG : (hh + 1) * SEG].astype(BF16)
        for peer in rep_peers:
            src = YB.at[s, half, peer[0]]
            send(src, YR.at[s, half, h], sx_s.at[9 + half, s], sx_r.at[9 + half, s], peer)
        YR[s, half, h] = YB[s, half, h]

    def branch_part(s, half):
        wait_bytes(YR.at[s, half, 0:3], sx_r.at[9 + half, s])
        parts = [YR[s, half, hh].astype(F32) for hh in range(4)]
        return ((parts[0] + parts[1]) + (parts[2] + parts[3])).astype(BF16)

    def share_part(half, part):
        BR[half, h] = part
        for peer in rep_peers:
            send(BR.at[half, h], BR.at[half, h], sx_s.at[11, half], sx_r.at[11, half], peer)

    def middle_rows(half):
        wait_bytes(BR.at[half, 0:3], sx_r.at[11, half])
        branch = jnp.concatenate([BR[half, hh] for hh in range(4)], axis=1).astype(F32)
        middle = (raw_packed[half * HALF_ROWS : (half + 1) * HALF_ROWS] + branch).astype(BF16)
        return dot(unpack, middle)

    def send_home(s, half, part):
        OB[s, 4 * half : 4 * half + 4] = dot(spread, part).astype(BF16).reshape(4, WIDE, SEG)

        @pl.when(c == half)
        def _():
            OR[s, t] = OB[s, t]
            for zz, peer in zip(z_steps, z_peers):
                send(OB.at[s, 4 * half + zz], OR.at[s, t], sx_s.at[12, s], sx_r.at[12, s], peer)

        @pl.when(c != half)
        def _():
            for zz in [z] + z_steps:
                peer = (h, at(y, zz, x, half))
                send(OB.at[s, 4 * half + zz], OR.at[s, t], sx_s.at[12, s], sx_r.at[12, s], peer)

    def store_home(s):
        wait_bytes(OR.at[s, 0:7], sx_r.at[12, s])
        perm_back = permutations()[1]
        for zz in range(4):
            both = jnp.concatenate([OR[s, zz], OR[s, 4 + zz]], axis=1)
            out[s, :, zz * 256 : (zz + 1) * 256] = dot(both, perm_back).astype(BF16)[0:OWN]

    cut_rows()
    incoming[0].wait()
    pl.semaphore_wait(barrier, len(everyone))
    send_across(0)
    send_plain(0)
    send_across(1)
    gains = local_gains()
    send_summed(0)
    send_plain(1)
    send_across(2)
    send_summed(1)
    send_plain(2)
    send_across(3)
    for copy in incoming[4:7]:
        copy.wait()
    refit(0)
    send_summed(2)
    send_plain(3)
    pass_on(0)
    refit(1)
    send_summed(3)
    send_across(4)
    send_plain(4)
    send_rows()
    send_across(5)
    send_plain(5)
    pass_on(1)
    refit(2)
    refit(3)
    pass_on(2)
    send_summed(4)
    pass_on(3)
    raw_packed, raw = first_rows()
    acts = (raw * gains[0]).astype(BF16)
    choice = [route_column(0, k) for k in range(2)]
    for half in range(2):
        send_squares(0, half, raw[half * HALF : (half + 1) * HALF])
    send_summed(5)
    for e in range(EXPERTS):
        gathered(e)
        first_product(e, acts, choice, 0, PADDED)
    for half in range(2):
        swap_cores(0, half)
    for half in range(2):
        sum_group(0, half)
    refit(4)
    refit(5)
    pass_on(4)

    a, b = iota((3 * HALF_ROWS, 4 * PACKED), 0), iota((3 * HALF_ROWS, 4 * PACKED), 1)
    to_block = jnp.where(a >= HALF_ROWS, 1, 0) + jnp.where(a >= 2 * HALF_ROWS, 1, 0)
    to_z = div_by(a - to_block * HALF_ROWS, OWN)
    row = a - to_block * HALF_ROWS - to_z * OWN
    from_z = jnp.where(b >= PACKED, 1, 0) + jnp.where(b >= 2 * PACKED, 1, 0) + jnp.where(b >= 3 * PACKED, 1, 0)
    pack = one_hot(b == from_z * PACKED + to_block * PAD + row)
    pack = jnp.where(from_z == to_z, pack, jnp.zeros_like(pack))
    unpack = pick(HALF, HALF_ROWS, PAD, OWN)
    spread = pick(4 * WIDE, HALF_ROWS, WIDE, OWN)
    ids_packed = dot(pick(ROWS, PADDED, OWN, PAD), RT[...].reshape(PADDED, 128).astype(BF16))

    def packed_choice(s, k, half):
        return ids_packed[half * HALF_ROWS : (half + 1) * HALF_ROWS, 2 * s + k : 2 * s + k + 1]

    def own_and_other(s, half):
        one, two = packed_choice(s, 0, half), packed_choice(s, 1, half)
        return jnp.where(c == 0, one, two), jnp.where(c == 0, two, one)

    def from_sums_to_parts(s):
        for half in range(2):
            hidden_units(s, half)
        if s == 0:
            gathered(4)
            gathered(5)
        totals = []
        for half in range(2):
            swap_hidden(s, half)
            totals.append(second_product(HB[s, half], own_and_other(s, half)[0], None))
        for half in range(2):
            wait_bytes(HO.at[s, half], sx_r.at[7 + half, s])
            send_sums(s, half, second_product(HO[s, half], own_and_other(s, half)[1], totals[half]))

    pass_on(5)
    from_sums_to_parts(0)
    parts = []
    for half in range(2):
        parts.append(branch_part(0, half))
        share_part(half, parts[half])
    for half in range(2):
        send_home(0, half, parts[half])
    for half in range(2):
        raw = middle_rows(half)
        acts = (raw * gains[1]).astype(BF16)
        choice = [route_column(1, k)[half * HALF : (half + 1) * HALF] for k in range(2)]
        for e in range(EXPERTS):
            first_product(e, acts, choice, half * HALF, HALF)
        swap_cores(1, half)
        send_squares(1, half, raw)
    for half in range(2):
        sum_group(1, half)
    from_sums_to_parts(1)
    store_home(0)
    for half in range(2):
        send_home(1, half, branch_part(1, half))
    store_home(1)

    for b in range(BATCHES):
        for way in range(2):
            wait_bytes(RA.at[b, way], sa_s.at[b, way])
            wait_bytes(RR.at[b, way], sr_s.at[b, way])
            where = pieces(b)
            pltpu.make_async_copy((N1, N2)[way].at[where], (new1, new2)[way].at[where], out_sem.at[b, way]).wait()
        for p in range(2):
            wait_bytes(W.at[b, p, 0, 0:3], ag_s.at[b, 0, p])
            wait_bytes(W.at[b, p, 0:3], ag_s.at[b, 1, p])
    wait_bytes(XS.at[0:7], sx_s.at[0, 0])
    wait_bytes(RT.at[0:7], st_s.at[0])
    for half in range(2):
        wait_bytes(BR.at[half, 0:3], sx_s.at[11, half])
    for s in range(2):
        for half in range(2):
            wait_bytes(SQR.at[s, half, 0:7], st_s.at[1 + 2 * s + half])
            wait_bytes(CR.at[s, half], sx_s.at[1 + half, s])
            wait_bytes(ZR.at[s, half, 0:3], sx_s.at[3 + half, s])
            wait_bytes(HB.at[s, half, 0:3], sx_s.at[5 + half, s])
            wait_bytes(HO.at[s, half], sx_s.at[7 + half, s])
            wait_bytes(YR.at[s, half, 0:3], sx_s.at[9 + half, s])
        wait_bytes(OR.at[s, 0:7], sx_s.at[12, s])


def shards(grad_stack, master_weight, moment_one, moment_two, decode_rows, norm_gain, route_ids, route_weights):
    dma = pltpu.SemaphoreType.DMA
    vmem = pltpu.VMEM
    scratch = [
        vmem((EXPERTS, 3, SLICE, 4 * HID), BF16),
        vmem((3, EXPERTS, 3, SLICE, HID), F32),
        vmem((EXPERTS, 3, SLICE, HID), F32),
        vmem((EXPERTS, 3, SLICE, HID), F32),
        vmem((BATCHES, 2, 4, 4, SLICE, HID), BF16),
        vmem((BATCHES, 2, 2, 16, HID), BF16),
        vmem((BATCHES, 2, 2, 16, HID), BF16),
        vmem((BATCHES, 2, 2, SLICE, HID), BF16),
        vmem((OWN, D), BF16),
        vmem((2, D), BF16),
        vmem((2, 2, OWN), jnp.int32),
        vmem((2, 2, OWN), F32),
        vmem((WIDE, D), BF16),
        vmem((GROUP, 4 * OWN, SEG), BF16),
        vmem((GROUP, 4 * OWN, SEG), BF16),
        vmem((GROUP, PAD, 128), F32),
        vmem((2, 2, PADDED, HID), F32),
        vmem((2, 2, 2, 2, HALF, HID), BF16),
        vmem((2, 2, 2, HALF, HID), BF16),
        vmem((2, 2, 4, BOTH, HID), BF16),
        vmem((2, 2, 4, BOTH, HID), BF16),
        vmem((2, 2, 4, 8, 128), F32),
        vmem((2, 2, GROUP, 8, 128), F32),
        vmem((2, 2, 4, PACKED, 128), BF16),
        vmem((2, 2, 4, PACKED, 128), BF16),
        vmem((2, 2, 4, HALF_ROWS, SEG), BF16),
        vmem((2, 2, 4, HALF_ROWS, SEG), BF16),
        vmem((2, 4, HALF_ROWS, SEG), BF16),
        vmem((2, GROUP, WIDE, SEG), BF16),
        vmem((2, GROUP, WIDE, SEG), BF16),
        dma((8,)),
        dma((BATCHES, 2)),
        dma((BATCHES, 2)),
        dma((BATCHES, 2)),
        dma((BATCHES, 2)),
        dma((BATCHES, 2)),
        dma((BATCHES, 2, 2)),
        dma((BATCHES, 2, 2)),
        dma((13, 2)),
        dma((13, 2)),
        dma((5,)),
        dma((5,)),
    ]
    in_vmem = pl.BlockSpec(memory_space=pltpu.VMEM)
    in_hbm = pl.BlockSpec(memory_space=pltpu.HBM)
    return pl.pallas_call(
        kernel,
        out_shape=(
            jax.ShapeDtypeStruct(moment_one.shape, F32),
            jax.ShapeDtypeStruct(moment_two.shape, F32),
            jax.ShapeDtypeStruct((2, OWN, D // 4), BF16),
        ),
        in_specs=[in_hbm] * 8,
        out_specs=(in_hbm, in_hbm, in_vmem),
        scratch_shapes=scratch,
        compiler_params=pltpu.CompilerParams(
            collective_id=0, has_side_effects=True, vmem_limit_bytes=62 * 1024 * 1024
        ),
        name="refit_and_decode",
    )(
        grad_stack,
        master_weight,
        moment_one,
        moment_two,
        decode_rows,
        norm_gain,
        route_ids.transpose(0, 2, 1),
        route_weights.transpose(0, 2, 1),
    )


def solution(mesh):
    return jax.shard_map(
        shards,
        mesh=mesh,
        in_specs=(
            P("rep", None, None, "shard", None),
            P(None, None, "shard", "rep"),
            P(None, None, "shard", "rep"),
            P(None, None, "shard", "rep"),
            P("shard", None),
            P(),
            P(None, "shard", None),
            P(None, "shard", None),
        ),
        out_specs=(
            P(None, None, "shard", "rep"),
            P(None, None, "shard", "rep"),
            P(None, "shard", "rep"),
        ),
        check_vma=False,
    )
```

```python
import jax
import jax.numpy as jnp
from jax import lax
from jax.experimental import pallas as pl
from jax.experimental.pallas import tpu as pltpu
from jax.sharding import PartitionSpec as P

beta_one = 0.9
beta_two = 0.95
learn_rate = 0.05
adam_eps = 1e-08
bias_one = 1.0 - 0.9**10
bias_two = 1.0 - 0.95**10

MESH = pl.DeviceIdType.MESH
F32 = jnp.float32
BF16 = jnp.bfloat16

EXPERTS = 4
D = 4096
SLICE = 32
HID = 384
OWN = 20
PAD = 24
WIDE = 32
GROUP = 8
ROWS = OWN * GROUP
PADDED = PAD * GROUP
HALF = PADDED // 2
HALF_ROWS = ROWS // 2
BOTH = 2 * PAD
PACKED = 80
LOCAL = 512
BATCHES = 6
SEG = 128


def div_by(value, count):
    scale = {20: 3277, 24: 2731}[count]
    return (value * scale) >> 16


def iota(shape, dim):
    return lax.broadcasted_iota(jnp.int32, shape, dim)


def one_hot(mask):
    return jnp.where(mask, 1.0, 0.0).astype(BF16)


def dot(a, b):
    return jnp.dot(a, b, preferred_element_type=F32)


def dot_last(a, b):
    return lax.dot_general(a, b, (((1,), (1,)), ((), ())), preferred_element_type=F32)


def wait_bytes(ref, sem):
    pltpu.make_async_copy(ref, ref, sem).wait()


def kernel(
    grads,
    master,
    mom1,
    mom2,
    rows,
    gain,
    ids,
    weights,
    new1,
    new2,
    out,
    GV,
    MV,
    N1,
    N2,
    W,
    RA,
    SB,
    RR,
    RV,
    GN,
    IV,
    WV,
    R32,
    XS,
    XR,
    RT,
    PA,
    PB,
    CR,
    TB,
    ZR,
    SQS,
    SQC,
    SQT,
    SQR,
    HB,
    HO,
    YB,
    YR,
    BR,
    OB,
    OR,
    in_sem,
    out_sem,
    sa_s,
    sa_r,
    sr_s,
    sr_r,
    ag_s,
    ag_r,
    sx_s,
    sx_r,
    st_s,
    st_r,
):
    h = lax.axis_index("rep")
    shard = lax.axis_index("shard")
    c = lax.rem(shard, 2)
    x = lax.rem(lax.div(shard, 2), 4)
    z = lax.rem(lax.div(shard, 8), 4)
    y = lax.div(shard, 32)
    t = c * 4 + z

    def at(yy, zz, xx, cc):
        return ((yy * 4 + zz) * 4 + xx) * 2 + cc

    def ahead(value, by):
        return lax.rem(value + by, 4)

    rep_peers = [(ahead(h, by), shard) for by in (1, 2, 3)]
    x_peers = [(h, at(y, z, ahead(x, by), c)) for by in (1, 2, 3)]
    y_peers = [(h, at(ahead(y, by), z, x, c)) for by in (1, 2, 3)]
    z_steps = [ahead(z, by) for by in (1, 2, 3)]
    z_peers = [(h, at(y, zz, x, c)) for zz in z_steps]
    core_peer = (h, at(y, z, x, 1 - c))
    group_steps = [(zz, c) for zz in z_steps]
    group_steps += [(zz, 1 - c) for zz in [z] + z_steps]
    group_peers = [(h, at(y, zz, x, cc)) for zz, cc in group_steps]

    place = 4 * h + z

    def near(by, cc):
        there = lax.rem(place + by + 16, 16)
        return (lax.div(there, 4), at(y, lax.rem(there, 4), x, cc))

    two = jnp.where(lax.rem(place, 2) == 0, 2, -2)
    near_steps = [(by, cc) for by in (1, -1, two) for cc in (0, 1)]

    def send(src, dst, s_sem, r_sem, to):
        pltpu.make_async_remote_copy(
            src_ref=src,
            dst_ref=dst,
            send_sem=s_sem,
            recv_sem=r_sem,
            device_id=to,
            device_id_type=MESH,
        ).start()

    barrier = pltpu.get_barrier_semaphore()
    everyone = rep_peers + x_peers + y_peers + group_peers
    everyone += [near(by, cc) for by in (1, -1, 2, -2) for cc in (0, 1)]
    for peer in everyone:
        pl.semaphore_signal(barrier, inc=1, device_id=peer, device_id_type=MESH)
    incoming = [
        pltpu.make_async_copy(grads.at[0], GV, in_sem.at[0]),
        pltpu.make_async_copy(rows, RV, in_sem.at[1]),
        pltpu.make_async_copy(gain, GN, in_sem.at[2]),
        pltpu.make_async_copy(ids, IV, in_sem.at[3]),
        pltpu.make_async_copy(master, MV.at[0], in_sem.at[4]),
        pltpu.make_async_copy(mom1, MV.at[1], in_sem.at[5]),
        pltpu.make_async_copy(mom2, MV.at[2], in_sem.at[6]),
        pltpu.make_async_copy(weights, WV, in_sem.at[7]),
    ]
    for copy in incoming:
        copy.start()

    def pick(n_to, n_from, to_len, from_len):
        a, b = iota((n_to, n_from), 0), iota((n_to, n_from), 1)
        ta = a >> 5 if to_len == 32 else div_by(a, to_len)
        tb = b >> 5 if from_len == 32 else div_by(b, from_len)
        ia, ib = a - ta * to_len, b - tb * from_len
        return one_hot((ta == tb) & (ia == ib) & (ia < OWN))

    hp, hm, h2 = ahead(h, 1), ahead(h, 3), ahead(h, 2)
    up_peer, down_peer = (hp, shard), (hm, shard)

    def columns(owner):
        return pl.ds(pl.multiple_of(owner * HID, HID), HID)

    def pieces(b):
        if b < 4:
            return (b, slice(0, 2))
        return (slice(2 * (b - 4), 2 * (b - 4) + 2), 2)

    def grad_at(b, first, last, owner):
        return (*pieces(b), slice(first, last), columns(owner))

    def send_across(b):
        send(GV.at[grad_at(b, 0, 16, h2)], RA.at[b, 0], sa_s.at[b, 0], sa_r.at[b, 0], up_peer)
        send(GV.at[grad_at(b, 16, 32, h2)], RA.at[b, 1], sa_s.at[b, 1], sa_r.at[b, 1], down_peer)

    def send_plain(b):
        src = GV.at[grad_at(b, 16, 32, hp)]
        send(src, RR.at[b, 0, :, 16:32], sr_s.at[b, 0], sr_r.at[b, 0], up_peer)
        src = GV.at[grad_at(b, 0, 16, hm)]
        send(src, RR.at[b, 1, :, 0:16], sr_s.at[b, 1], sr_r.at[b, 1], down_peer)

    def send_summed(b):
        wait_bytes(RA.at[b, 0], sa_r.at[b, 0])
        SB[b, 0] = (RA[b, 0].astype(F32) + GV[grad_at(b, 0, 16, hp)].astype(F32)).astype(BF16)
        send(SB.at[b, 0], RR.at[b, 0, :, 0:16], sr_s.at[b, 0], sr_r.at[b, 0], up_peer)
        wait_bytes(RA.at[b, 1], sa_r.at[b, 1])
        SB[b, 1] = (RA[b, 1].astype(F32) + GV[grad_at(b, 16, 32, hm)].astype(F32)).astype(BF16)
        send(SB.at[b, 1], RR.at[b, 1, :, 16:32], sr_s.at[b, 1], sr_r.at[b, 1], down_peer)

    def refit(b):
        wait_bytes(RR.at[b, 0], sr_r.at[b, 0])
        wait_bytes(RR.at[b, 1], sr_r.at[b, 1])
        total = GV[grad_at(b, 0, 32, h)].astype(F32) + RR[b, 0].astype(F32) + RR[b, 1].astype(F32)
        mean = total * 0.25
        where = pieces(b)
        one = beta_one * MV[(1, *where)] + (1.0 - beta_one) * mean
        two = beta_two * MV[(2, *where)] + (1.0 - beta_two) * mean * mean
        update = one / bias_one / (jnp.sqrt(two / bias_two) + adam_eps)
        W[b, :, y, x] = (MV[(0, *where)] - learn_rate * update).astype(BF16)
        for peer in x_peers:
            send(W.at[b, 0, y, x], W.at[b, 0, y, x], ag_s.at[b, 0, 0], ag_r.at[b, 0, 0], peer)
        for peer in y_peers:
            send(W.at[b, 1, y, x], W.at[b, 1, y, x], ag_s.at[b, 0, 1], ag_r.at[b, 0, 1], peer)
        N1[where] = one
        N2[where] = two
        pltpu.make_async_copy(N1.at[where], new1.at[where], out_sem.at[b, 0]).start()
        pltpu.make_async_copy(N2.at[where], new2.at[where], out_sem.at[b, 1]).start()

    def pass_on(b):
        wait_bytes(W.at[b, 0, 0, 0:3], ag_r.at[b, 0, 0])
        for peer in y_peers:
            send(W.at[b, 0, y], W.at[b, 0, y], ag_s.at[b, 1, 0], ag_r.at[b, 1, 0], peer)
        wait_bytes(W.at[b, 1, 0, 0:3], ag_r.at[b, 0, 1])
        for peer in x_peers:
            send(W.at[b, 1, :, x], W.at[b, 1, :, x], ag_s.at[b, 1, 1], ag_r.at[b, 1, 1], peer)

    def gathered(b):
        wait_bytes(W.at[b, 0, 0:3], ag_r.at[b, 1, 0])
        wait_bytes(W.at[b, 1, 0:3], ag_r.at[b, 1, 1])

    def permutations():
        q = iota((256, 256), 1)
        r = iota((256, 256), 0)
        q_src = ((q & 127) >> 5) * 64 + (q >> 7) * 32 + (q & 31)
        r_src = ((r & 127) >> 5) * 64 + (r >> 7) * 32 + (r & 31)
        return one_hot(r == q_src), one_hot(q == r_src)

    def cut_rows():
        R32[...] = jnp.zeros(R32.shape, BF16)
        perm = permutations()[0]
        incoming[3].wait()
        incoming[7].wait()
        diagonal = iota((PAD, OWN), 0) == iota((PAD, OWN), 1)
        lane = iota((PAD, 128), 1)
        tile = jnp.zeros((PAD, 128), F32)
        for s in range(2):
            for k in range(2):
                for first, line in ((0, IV[s, k : k + 1].astype(F32)), (4, WV[s, k : k + 1])):
                    column = jnp.sum(jnp.where(diagonal, line, 0.0), axis=1, keepdims=True)
                    tile = jnp.where(lane == first + 2 * s + k, column, tile)
        RT[t] = tile
        incoming[1].wait()
        R32[0:OWN, :] = RV[...]
        blocks = [R32[:, (4 * yy + zz) * 256 : (4 * yy + zz + 1) * 256] for zz in range(4) for yy in range(4)]
        moved = dot(jnp.concatenate(blocks, axis=0), perm).astype(BF16)
        moved = dot(pick(16 * OWN, 16 * WIDE, OWN, WIDE), moved).astype(BF16)
        for zz in range(4):
            XS[zz] = moved[4 * zz * OWN : 4 * (zz + 1) * OWN, 0:SEG]
            XS[4 + zz] = moved[4 * zz * OWN : 4 * (zz + 1) * OWN, SEG : 2 * SEG]
        XR[t] = XS[t]

    def send_rows():
        for by, cc in near_steps:
            zz = lax.rem(place + by + 16, 4)
            send(XS.at[4 * cc + zz], XR.at[t], sx_s.at[0, 0], sx_r.at[0, 0], near(by, cc))
            send(RT.at[t], RT.at[t], st_s.at[0], st_r.at[0], near(by, cc))
        send(XS.at[4 * (1 - c) + z], XR.at[t], sx_s.at[0, 0], sx_r.at[0, 0], core_peer)
        send(RT.at[t], RT.at[t], st_s.at[0], st_r.at[0], core_peer)

    def local_gains():
        incoming[2].wait()
        perm = permutations()[0]
        gains = [[], []]
        for yy in range(4):
            first = pl.multiple_of(yy * 1024 + z * 256, 256)
            both = dot(GN[:, pl.ds(first, 256)], perm)
            both = jnp.where(c == 0, both[:, 0:SEG], both[:, SEG : 2 * SEG])
            for s in range(2):
                gains[s].append(both[s : s + 1])
        return [jnp.concatenate(parts, axis=1) for parts in gains]

    def first_rows():
        wait_bytes(XR.at[0:7], sx_r.at[0, 0])
        wait_bytes(RT.at[0:7], st_r.at[0])
        a, b = iota((4 * ROWS, 4 * ROWS), 0), iota((4 * ROWS, 4 * ROWS), 1)
        to_y = sum(jnp.where(a >= n * ROWS, 1, 0) for n in (1, 2, 3))
        to_t = div_by(a - to_y * ROWS, OWN)
        source = to_t * (4 * OWN) + to_y * OWN + (a - to_y * ROWS - to_t * OWN)
        arrived = dot(one_hot(b == source), XR[...].reshape(4 * ROWS, SEG))
        raw_packed = jnp.concatenate([arrived[n * ROWS : (n + 1) * ROWS] for n in range(4)], axis=1)
        raw = dot(pick(PADDED, ROWS, PAD, OWN), raw_packed.astype(BF16))
        return raw_packed, raw

    def route_column(s, k):
        return RT[...].reshape(PADDED, 128)[:, 2 * s + k : 2 * s + k + 1]

    same = iota((PAD, 128), 0) == iota((PAD, 128), 1)

    def send_squares(s, half, raw):
        squares = jnp.sum(raw * raw, axis=1, keepdims=True)
        for zz in range(4):
            part = squares[zz * PAD : (zz + 1) * PAD]
            line = jnp.sum(jnp.where(same, part, 0.0), axis=0, keepdims=True)
            SQS[s, half, zz] = jnp.broadcast_to(line, (8, 128))
        n = 1 + 2 * s + half
        send(SQS.at[s, half], SQC.at[s, half], st_s.at[n], st_r.at[n], core_peer)

    def first_product(e, activations, choice, first, count):
        gate = dot(activations, W[e, 0].reshape(LOCAL, HID))
        up = dot(activations, W[e, 1].reshape(LOCAL, HID))
        for k in range(2):
            chosen = choice[k] == float(e)
            for g, value in enumerate((gate, up)):
                value = jnp.where(chosen, value, 0.0)
                if e > 0:
                    value = PA[k, g, first : first + count] + value
                PA[k, g, first : first + count] = value

    def swap_cores(s, half):
        for k in range(2):
            for g in range(2):
                PB[s, half, k, g] = PA[k, g, half * HALF : (half + 1) * HALF].astype(BF16)
        send(PB.at[s, half, 1 - c], CR.at[s, half], sx_s.at[1 + half, s], sx_r.at[1 + half, s], core_peer)

    def sum_group(s, half):
        wait_bytes(SQC.at[s, half], st_r.at[1 + 2 * s + half])
        SQT[s, half] = SQS[s, half] + SQC[s, half]
        n = 5 + 2 * s + half
        for zz, peer in zip(z_steps, z_peers):
            send(SQT.at[s, half, zz], SQR.at[s, half, z], st_s.at[n], st_r.at[n], peer)
        SQR[s, half, z] = SQT[s, half, z]
        wait_bytes(CR.at[s, half], sx_r.at[1 + half, s])
        gate = PB[s, half, c, 0].astype(F32) + CR[s, half, 0].astype(F32)
        up = PB[s, half, c, 1].astype(F32) + CR[s, half, 1].astype(F32)
        for zz in range(4):
            cut = slice(zz * PAD, (zz + 1) * PAD)
            TB[s, half, zz] = jnp.concatenate([gate[cut], up[cut]], axis=0).astype(BF16)
        for zz, peer in zip(z_steps, z_peers):
            send(TB.at[s, half, zz], ZR.at[s, half, z], sx_s.at[3 + half, s], sx_r.at[3 + half, s], peer)
        ZR[s, half, z] = TB[s, half, z]

    def hidden_units(s, half):
        wait_bytes(SQR.at[s, half, 0:3], st_r.at[5 + 2 * s + half])
        total = jnp.sum(SQR[s, half][:, 0, :], axis=0, keepdims=True)
        scale_line = lax.rsqrt(total / float(D) + 1e-06)
        scale = jnp.sum(jnp.where(same, scale_line, 0.0), axis=1, keepdims=True)
        routes = RT[4 * half + z]
        share = jnp.where(c == 0, routes[:, 4 + 2 * s : 5 + 2 * s], routes[:, 5 + 2 * s : 6 + 2 * s])
        wait_bytes(ZR.at[s, half, 0:3], sx_r.at[3 + half, s])
        parts = [ZR[s, half, zz].astype(F32) for zz in range(4)]
        both = (parts[0] + parts[1]) + (parts[2] + parts[3])
        gate, up = both[0:PAD] * scale, both[PAD:BOTH] * scale
        units = jax.nn.silu(gate) * up * share
        blocks = [units[:, i * 128 : (i + 1) * 128] for i in range(3)]
        blocks.append(jnp.zeros((PACKED - 3 * PAD, 128), F32))
        HB[s, half, z] = jnp.concatenate(blocks, axis=0).astype(BF16)
        for peer in z_peers:
            send(HB.at[s, half, z], HB.at[s, half, z], sx_s.at[5 + half, s], sx_r.at[5 + half, s], peer)

    def swap_hidden(s, half):
        wait_bytes(HB.at[s, half, 0:3], sx_r.at[5 + half, s])
        send(HB.at[s, half], HO.at[s, half], sx_s.at[7 + half, s], sx_r.at[7 + half, s], core_peer)

    def second_product(units, choice, total):
        flat = dot(pack, units.reshape(4 * PACKED, 128))
        flat = jnp.concatenate([flat[i * HALF_ROWS : (i + 1) * HALF_ROWS] for i in range(3)], axis=1)
        for e in range(EXPERTS):
            mine = jnp.where(choice == float(e), flat, 0.0).astype(BF16)
            part = dot_last(mine, W[4 + e // 2, e % 2].reshape(LOCAL, HID))
            total = part if total is None else total + part
        return total

    def send_sums(s, half, total):
        for hh in range(4):
            YB[s, half, hh] = total[:, hh * SEG : (hh + 1) * SEG].astype(BF16)
        for peer in rep_peers:
            src = YB.at[s, half, peer[0]]
            send(src, YR.at[s, half, h], sx_s.at[9 + half, s], sx_r.at[9 + half, s], peer)
        YR[s, half, h] = YB[s, half, h]

    def branch_part(s, half):
        wait_bytes(YR.at[s, half, 0:3], sx_r.at[9 + half, s])
        parts = [YR[s, half, hh].astype(F32) for hh in range(4)]
        return ((parts[0] + parts[1]) + (parts[2] + parts[3])).astype(BF16)

    def share_part(half, part):
        BR[half, h] = part
        for peer in rep_peers:
            send(BR.at[half, h], BR.at[half, h], sx_s.at[11, half], sx_r.at[11, half], peer)

    def middle_rows(half):
        wait_bytes(BR.at[half, 0:3], sx_r.at[11, half])
        branch = jnp.concatenate([BR[half, hh] for hh in range(4)], axis=1).astype(F32)
        middle = (raw_packed[half * HALF_ROWS : (half + 1) * HALF_ROWS] + branch).astype(BF16)
        return dot(unpack, middle)

    def send_home(s, half, part):
        OB[s, 4 * half : 4 * half + 4] = dot(spread, part).astype(BF16).reshape(4, WIDE, SEG)

        @pl.when(c == half)
        def _():
            OR[s, t] = OB[s, t]
            for zz, peer in zip(z_steps, z_peers):
                send(OB.at[s, 4 * half + zz], OR.at[s, t], sx_s.at[12, s], sx_r.at[12, s], peer)

        @pl.when(c != half)
        def _():
            for zz in [z] + z_steps:
                peer = (h, at(y, zz, x, half))
                send(OB.at[s, 4 * half + zz], OR.at[s, t], sx_s.at[12, s], sx_r.at[12, s], peer)

    def store_home(s):
        wait_bytes(OR.at[s, 0:7], sx_r.at[12, s])
        perm_back = permutations()[1]
        for zz in range(4):
            both = jnp.concatenate([OR[s, zz], OR[s, 4 + zz]], axis=1)
            out[s, :, zz * 256 : (zz + 1) * 256] = dot(both, perm_back).astype(BF16)[0:OWN]

    cut_rows()
    incoming[0].wait()
    pl.semaphore_wait(barrier, len(everyone))
    send_across(0)
    send_plain(0)
    send_across(1)
    gains = local_gains()
    send_summed(0)
    send_plain(1)
    send_across(2)
    send_summed(1)
    send_plain(2)
    send_across(3)
    for copy in incoming[4:7]:
        copy.wait()
    refit(0)
    send_summed(2)
    send_plain(3)
    pass_on(0)
    refit(1)
    send_summed(3)
    send_across(4)
    send_plain(4)
    send_rows()
    send_across(5)
    send_plain(5)
    pass_on(1)
    refit(2)
    refit(3)
    pass_on(2)
    send_summed(4)
    pass_on(3)
    raw_packed, raw = first_rows()
    acts = (raw * gains[0]).astype(BF16)
    choice = [route_column(0, k) for k in range(2)]
    for half in range(2):
        send_squares(0, half, raw[half * HALF : (half + 1) * HALF])
    send_summed(5)
    for e in range(EXPERTS):
        gathered(e)
        first_product(e, acts, choice, 0, PADDED)
    for half in range(2):
        swap_cores(0, half)
    for half in range(2):
        sum_group(0, half)
    refit(4)
    refit(5)
    pass_on(4)

    a, b = iota((3 * HALF_ROWS, 4 * PACKED), 0), iota((3 * HALF_ROWS, 4 * PACKED), 1)
    to_block = jnp.where(a >= HALF_ROWS, 1, 0) + jnp.where(a >= 2 * HALF_ROWS, 1, 0)
    to_z = div_by(a - to_block * HALF_ROWS, OWN)
    row = a - to_block * HALF_ROWS - to_z * OWN
    from_z = jnp.where(b >= PACKED, 1, 0) + jnp.where(b >= 2 * PACKED, 1, 0) + jnp.where(b >= 3 * PACKED, 1, 0)
    pack = one_hot(b == from_z * PACKED + to_block * PAD + row)
    pack = jnp.where(from_z == to_z, pack, jnp.zeros_like(pack))
    unpack = pick(HALF, HALF_ROWS, PAD, OWN)
    spread = pick(4 * WIDE, HALF_ROWS, WIDE, OWN)
    ids_packed = dot(pick(ROWS, PADDED, OWN, PAD), RT[...].reshape(PADDED, 128).astype(BF16))

    def packed_choice(s, k, half):
        return ids_packed[half * HALF_ROWS : (half + 1) * HALF_ROWS, 2 * s + k : 2 * s + k + 1]

    def own_and_other(s, half):
        one, two = packed_choice(s, 0, half), packed_choice(s, 1, half)
        return jnp.where(c == 0, one, two), jnp.where(c == 0, two, one)

    def from_sums_to_parts(s):
        for half in range(2):
            hidden_units(s, half)
        if s == 0:
            gathered(4)
            gathered(5)
        for half in range(2):
            own, other = own_and_other(s, half)
            swap_hidden(s, half)
            total = second_product(HB[s, half], own, None)
            wait_bytes(HO.at[s, half], sx_r.at[7 + half, s])
            send_sums(s, half, second_product(HO[s, half], other, total))

    pass_on(5)
    from_sums_to_parts(0)
    parts = []
    for half in range(2):
        parts.append(branch_part(0, half))
        share_part(half, parts[half])
    for half in range(2):
        send_home(0, half, parts[half])
    for half in range(2):
        raw = middle_rows(half)
        acts = (raw * gains[1]).astype(BF16)
        choice = [route_column(1, k)[half * HALF : (half + 1) * HALF] for k in range(2)]
        for e in range(EXPERTS):
            first_product(e, acts, choice, half * HALF, HALF)
        swap_cores(1, half)
        send_squares(1, half, raw)
        sum_group(1, half)
    from_sums_to_parts(1)
    store_home(0)
    for half in range(2):
        send_home(1, half, branch_part(1, half))
    store_home(1)

    for b in range(BATCHES):
        for way in range(2):
            wait_bytes(RA.at[b, way], sa_s.at[b, way])
            wait_bytes(RR.at[b, way], sr_s.at[b, way])
            where = pieces(b)
            pltpu.make_async_copy((N1, N2)[way].at[where], (new1, new2)[way].at[where], out_sem.at[b, way]).wait()
        for p in range(2):
            wait_bytes(W.at[b, p, 0, 0:3], ag_s.at[b, 0, p])
            wait_bytes(W.at[b, p, 0:3], ag_s.at[b, 1, p])
    wait_bytes(XS.at[0:7], sx_s.at[0, 0])
    wait_bytes(RT.at[0:7], st_s.at[0])
    for half in range(2):
        wait_bytes(BR.at[half, 0:3], sx_s.at[11, half])
    for s in range(2):
        for half in range(2):
            wait_bytes(SQC.at[s, half], st_s.at[1 + 2 * s + half])
            wait_bytes(SQR.at[s, half, 0:3], st_s.at[5 + 2 * s + half])
            wait_bytes(CR.at[s, half], sx_s.at[1 + half, s])
            wait_bytes(ZR.at[s, half, 0:3], sx_s.at[3 + half, s])
            wait_bytes(HB.at[s, half, 0:3], sx_s.at[5 + half, s])
            wait_bytes(HO.at[s, half], sx_s.at[7 + half, s])
            wait_bytes(YR.at[s, half, 0:3], sx_s.at[9 + half, s])
        wait_bytes(OR.at[s, 0:7], sx_s.at[12, s])


def shards(grad_stack, master_weight, moment_one, moment_two, decode_rows, norm_gain, route_ids, route_weights):
    dma = pltpu.SemaphoreType.DMA
    vmem = pltpu.VMEM
    scratch = [
        vmem((EXPERTS, 3, SLICE, 4 * HID), BF16),
        vmem((3, EXPERTS, 3, SLICE, HID), F32),
        vmem((EXPERTS, 3, SLICE, HID), F32),
        vmem((EXPERTS, 3, SLICE, HID), F32),
        vmem((BATCHES, 2, 4, 4, SLICE, HID), BF16),
        vmem((BATCHES, 2, 2, 16, HID), BF16),
        vmem((BATCHES, 2, 2, 16, HID), BF16),
        vmem((BATCHES, 2, 2, SLICE, HID), BF16),
        vmem((OWN, D), BF16),
        vmem((2, D), BF16),
        vmem((2, 2, OWN), jnp.int32),
        vmem((2, 2, OWN), F32),
        vmem((WIDE, D), BF16),
        vmem((GROUP, 4 * OWN, SEG), BF16),
        vmem((GROUP, 4 * OWN, SEG), BF16),
        vmem((GROUP, PAD, 128), F32),
        vmem((2, 2, PADDED, HID), F32),
        vmem((2, 2, 2, 2, HALF, HID), BF16),
        vmem((2, 2, 2, HALF, HID), BF16),
        vmem((2, 2, 4, BOTH, HID), BF16),
        vmem((2, 2, 4, BOTH, HID), BF16),
        vmem((2, 2, 4, 8, 128), F32),
        vmem((2, 2, 4, 8, 128), F32),
        vmem((2, 2, 4, 8, 128), F32),
        vmem((2, 2, 4, 8, 128), F32),
        vmem((2, 2, 4, PACKED, 128), BF16),
        vmem((2, 2, 4, PACKED, 128), BF16),
        vmem((2, 2, 4, HALF_ROWS, SEG), BF16),
        vmem((2, 2, 4, HALF_ROWS, SEG), BF16),
        vmem((2, 4, HALF_ROWS, SEG), BF16),
        vmem((2, GROUP, WIDE, SEG), BF16),
        vmem((2, GROUP, WIDE, SEG), BF16),
        dma((8,)),
        dma((BATCHES, 2)),
        dma((BATCHES, 2)),
        dma((BATCHES, 2)),
        dma((BATCHES, 2)),
        dma((BATCHES, 2)),
        dma((BATCHES, 2, 2)),
        dma((BATCHES, 2, 2)),
        dma((13, 2)),
        dma((13, 2)),
        dma((9,)),
        dma((9,)),
    ]
    in_vmem = pl.BlockSpec(memory_space=pltpu.VMEM)
    in_hbm = pl.BlockSpec(memory_space=pltpu.HBM)
    return pl.pallas_call(
        kernel,
        out_shape=(
            jax.ShapeDtypeStruct(moment_one.shape, F32),
            jax.ShapeDtypeStruct(moment_two.shape, F32),
            jax.ShapeDtypeStruct((2, OWN, D // 4), BF16),
        ),
        in_specs=[in_hbm] * 8,
        out_specs=(in_hbm, in_hbm, in_vmem),
        scratch_shapes=scratch,
        compiler_params=pltpu.CompilerParams(
            collective_id=0, has_side_effects=True, vmem_limit_bytes=62 * 1024 * 1024
        ),
        name="refit_and_decode",
    )(
        grad_stack,
        master_weight,
        moment_one,
        moment_two,
        decode_rows,
        norm_gain,
        route_ids.transpose(0, 2, 1),
        route_weights.transpose(0, 2, 1),
    )


def solution(mesh):
    return jax.shard_map(
        shards,
        mesh=mesh,
        in_specs=(
            P("rep", None, None, "shard", None),
            P(None, None, "shard", "rep"),
            P(None, None, "shard", "rep"),
            P(None, None, "shard", "rep"),
            P("shard", None),
            P(),
            P(None, "shard", None),
            P(None, "shard", None),
        ),
        out_specs=(
            P(None, None, "shard", "rep"),
            P(None, None, "shard", "rep"),
            P(None, "shard", "rep"),
        ),
        check_vma=False,
    )
```

```python
import jax
import jax.numpy as jnp
from jax import lax
from jax.experimental import pallas as pl
from jax.experimental.pallas import tpu as pltpu
from jax.sharding import PartitionSpec as P

beta_one = 0.9
beta_two = 0.95
learn_rate = 0.05
adam_eps = 1e-08
bias_one = 1.0 - 0.9**10
bias_two = 1.0 - 0.95**10

MESH = pl.DeviceIdType.MESH
F32 = jnp.float32
BF16 = jnp.bfloat16

EXPERTS = 4
D = 4096
SLICE = 32
HID = 384
OWN = 20
PAD = 24
WIDE = 32
GROUP = 8
ROWS = OWN * GROUP
PADDED = PAD * GROUP
HALF = PADDED // 2
HALF_ROWS = ROWS // 2
BOTH = 2 * PAD
PACKED = 80
LOCAL = 512
BATCHES = 6
SEG = 128


def div_by(value, count):
    scale = {20: 3277, 24: 2731}[count]
    return (value * scale) >> 16


def iota(shape, dim):
    return lax.broadcasted_iota(jnp.int32, shape, dim)


def one_hot(mask):
    return jnp.where(mask, 1.0, 0.0).astype(BF16)


def dot(a, b):
    return jnp.dot(a, b, preferred_element_type=F32)


def dot_last(a, b):
    return lax.dot_general(a, b, (((1,), (1,)), ((), ())), preferred_element_type=F32)


def wait_bytes(ref, sem):
    pltpu.make_async_copy(ref, ref, sem).wait()


def kernel(
    grads,
    master,
    mom1,
    mom2,
    rows,
    gain,
    ids,
    weights,
    new1,
    new2,
    out,
    GV,
    MV,
    N1,
    N2,
    W,
    RA,
    SB,
    RR,
    RV,
    GN,
    IV,
    WV,
    R32,
    XS,
    XR,
    RT,
    PA,
    PB,
    CR,
    TB,
    ZR,
    SQS,
    SQC,
    SQT,
    SQR,
    HB,
    HO,
    YB,
    YR,
    BR,
    OB,
    OR,
    in_sem,
    out_sem,
    sa_s,
    sa_r,
    sr_s,
    sr_r,
    ag_s,
    ag_r,
    sx_s,
    sx_r,
    st_s,
    st_r,
):
    h = lax.axis_index("rep")
    shard = lax.axis_index("shard")
    c = lax.rem(shard, 2)
    x = lax.rem(lax.div(shard, 2), 4)
    z = lax.rem(lax.div(shard, 8), 4)
    y = lax.div(shard, 32)
    t = c * 4 + z

    def at(yy, zz, xx, cc):
        return ((yy * 4 + zz) * 4 + xx) * 2 + cc

    def ahead(value, by):
        return lax.rem(value + by, 4)

    rep_peers = [(ahead(h, by), shard) for by in (2, 1, 3)]
    x_peers = [(h, at(y, z, ahead(x, by), c)) for by in (1, 2, 3)]
    y_peers = [(h, at(ahead(y, by), z, x, c)) for by in (1, 2, 3)]
    z_steps = [ahead(z, by) for by in (1, 2, 3)]
    z_peers = [(h, at(y, zz, x, c)) for zz in z_steps]
    core_peer = (h, at(y, z, x, 1 - c))
    group_steps = [(zz, c) for zz in z_steps]
    group_steps += [(zz, 1 - c) for zz in [z] + z_steps]
    group_peers = [(h, at(y, zz, x, cc)) for zz, cc in group_steps]

    place = 4 * h + z

    def near(by, cc):
        there = lax.rem(place + by + 16, 16)
        return (lax.div(there, 4), at(y, lax.rem(there, 4), x, cc))

    two = jnp.where(lax.rem(place, 2) == 0, 2, -2)
    near_steps = [(by, cc) for by in (1, -1, two) for cc in (0, 1)]

    def send(src, dst, s_sem, r_sem, to):
        pltpu.make_async_remote_copy(
            src_ref=src,
            dst_ref=dst,
            send_sem=s_sem,
            recv_sem=r_sem,
            device_id=to,
            device_id_type=MESH,
        ).start()

    barrier = pltpu.get_barrier_semaphore()
    everyone = rep_peers + x_peers + y_peers + group_peers
    everyone += [near(by, cc) for by in (1, -1, 2, -2) for cc in (0, 1)]
    for peer in everyone:
        pl.semaphore_signal(barrier, inc=1, device_id=peer, device_id_type=MESH)
    incoming = [
        pltpu.make_async_copy(grads.at[0], GV, in_sem.at[0]),
        pltpu.make_async_copy(rows, RV, in_sem.at[1]),
        pltpu.make_async_copy(gain, GN, in_sem.at[2]),
        pltpu.make_async_copy(ids, IV, in_sem.at[3]),
        pltpu.make_async_copy(master, MV.at[0], in_sem.at[4]),
        pltpu.make_async_copy(mom1, MV.at[1], in_sem.at[5]),
        pltpu.make_async_copy(mom2, MV.at[2], in_sem.at[6]),
        pltpu.make_async_copy(weights, WV, in_sem.at[7]),
    ]
    for copy in incoming:
        copy.start()

    def pick(n_to, n_from, to_len, from_len):
        a, b = iota((n_to, n_from), 0), iota((n_to, n_from), 1)
        ta = a >> 5 if to_len == 32 else div_by(a, to_len)
        tb = b >> 5 if from_len == 32 else div_by(b, from_len)
        ia, ib = a - ta * to_len, b - tb * from_len
        return one_hot((ta == tb) & (ia == ib) & (ia < OWN))

    hp, hm, h2 = ahead(h, 1), ahead(h, 3), ahead(h, 2)
    up_peer, down_peer = (hp, shard), (hm, shard)

    def columns(owner):
        return pl.ds(pl.multiple_of(owner * HID, HID), HID)

    def pieces(b):
        if b < 4:
            return (b, slice(0, 2))
        return (slice(2 * (b - 4), 2 * (b - 4) + 2), 2)

    def grad_at(b, first, last, owner):
        return (*pieces(b), slice(first, last), columns(owner))

    def send_across(b):
        send(GV.at[grad_at(b, 0, 16, h2)], RA.at[b, 0], sa_s.at[b, 0], sa_r.at[b, 0], up_peer)
        send(GV.at[grad_at(b, 16, 32, h2)], RA.at[b, 1], sa_s.at[b, 1], sa_r.at[b, 1], down_peer)

    def send_plain(b):
        src = GV.at[grad_at(b, 16, 32, hp)]
        send(src, RR.at[b, 0, :, 16:32], sr_s.at[b, 0], sr_r.at[b, 0], up_peer)
        src = GV.at[grad_at(b, 0, 16, hm)]
        send(src, RR.at[b, 1, :, 0:16], sr_s.at[b, 1], sr_r.at[b, 1], down_peer)

    def send_summed(b):
        wait_bytes(RA.at[b, 0], sa_r.at[b, 0])
        SB[b, 0] = (RA[b, 0].astype(F32) + GV[grad_at(b, 0, 16, hp)].astype(F32)).astype(BF16)
        send(SB.at[b, 0], RR.at[b, 0, :, 0:16], sr_s.at[b, 0], sr_r.at[b, 0], up_peer)
        wait_bytes(RA.at[b, 1], sa_r.at[b, 1])
        SB[b, 1] = (RA[b, 1].astype(F32) + GV[grad_at(b, 16, 32, hm)].astype(F32)).astype(BF16)
        send(SB.at[b, 1], RR.at[b, 1, :, 16:32], sr_s.at[b, 1], sr_r.at[b, 1], down_peer)

    def refit(b):
        wait_bytes(RR.at[b, 0], sr_r.at[b, 0])
        wait_bytes(RR.at[b, 1], sr_r.at[b, 1])
        total = GV[grad_at(b, 0, 32, h)].astype(F32) + RR[b, 0].astype(F32) + RR[b, 1].astype(F32)
        mean = total * 0.25
        where = pieces(b)
        one = beta_one * MV[(1, *where)] + (1.0 - beta_one) * mean
        two = beta_two * MV[(2, *where)] + (1.0 - beta_two) * mean * mean
        update = one / bias_one / (jnp.sqrt(two / bias_two) + adam_eps)
        W[b, :, y, x] = (MV[(0, *where)] - learn_rate * update).astype(BF16)
        for peer in x_peers:
            send(W.at[b, 0, y, x], W.at[b, 0, y, x], ag_s.at[b, 0, 0], ag_r.at[b, 0, 0], peer)
        for peer in y_peers:
            send(W.at[b, 1, y, x], W.at[b, 1, y, x], ag_s.at[b, 0, 1], ag_r.at[b, 0, 1], peer)
        N1[where] = one
        N2[where] = two
        pltpu.make_async_copy(N1.at[where], new1.at[where], out_sem.at[b, 0]).start()
        pltpu.make_async_copy(N2.at[where], new2.at[where], out_sem.at[b, 1]).start()

    def pass_on(b):
        wait_bytes(W.at[b, 0, 0, 0:3], ag_r.at[b, 0, 0])
        for peer in y_peers:
            send(W.at[b, 0, y], W.at[b, 0, y], ag_s.at[b, 1, 0], ag_r.at[b, 1, 0], peer)
        wait_bytes(W.at[b, 1, 0, 0:3], ag_r.at[b, 0, 1])
        for peer in x_peers:
            send(W.at[b, 1, :, x], W.at[b, 1, :, x], ag_s.at[b, 1, 1], ag_r.at[b, 1, 1], peer)

    def gathered(b):
        wait_bytes(W.at[b, 0, 0:3], ag_r.at[b, 1, 0])
        wait_bytes(W.at[b, 1, 0:3], ag_r.at[b, 1, 1])

    def permutations():
        q = iota((256, 256), 1)
        r = iota((256, 256), 0)
        q_src = ((q & 127) >> 5) * 64 + (q >> 7) * 32 + (q & 31)
        r_src = ((r & 127) >> 5) * 64 + (r >> 7) * 32 + (r & 31)
        return one_hot(r == q_src), one_hot(q == r_src)

    def cut_rows():
        R32[...] = jnp.zeros(R32.shape, BF16)
        perm = permutations()[0]
        incoming[3].wait()
        incoming[7].wait()
        diagonal = iota((PAD, OWN), 0) == iota((PAD, OWN), 1)
        lane = iota((PAD, 128), 1)
        tile = jnp.zeros((PAD, 128), F32)
        for s in range(2):
            for k in range(2):
                for first, line in ((0, IV[s, k : k + 1].astype(F32)), (4, WV[s, k : k + 1])):
                    column = jnp.sum(jnp.where(diagonal, line, 0.0), axis=1, keepdims=True)
                    tile = jnp.where(lane == first + 2 * s + k, column, tile)
        RT[t] = tile
        incoming[1].wait()
        R32[0:OWN, :] = RV[...]
        blocks = [R32[:, (4 * yy + zz) * 256 : (4 * yy + zz + 1) * 256] for zz in range(4) for yy in range(4)]
        moved = dot(jnp.concatenate(blocks, axis=0), perm).astype(BF16)
        moved = dot(pick(16 * OWN, 16 * WIDE, OWN, WIDE), moved).astype(BF16)
        for zz in range(4):
            XS[zz] = moved[4 * zz * OWN : 4 * (zz + 1) * OWN, 0:SEG]
            XS[4 + zz] = moved[4 * zz * OWN : 4 * (zz + 1) * OWN, SEG : 2 * SEG]
        XR[t] = XS[t]

    def send_rows():
        for by, cc in near_steps:
            zz = lax.rem(place + by + 16, 4)
            send(XS.at[4 * cc + zz], XR.at[t], sx_s.at[0, 0], sx_r.at[0, 0], near(by, cc))
            send(RT.at[t], RT.at[t], st_s.at[0], st_r.at[0], near(by, cc))
        send(XS.at[4 * (1 - c) + z], XR.at[t], sx_s.at[0, 0], sx_r.at[0, 0], core_peer)
        send(RT.at[t], RT.at[t], st_s.at[0], st_r.at[0], core_peer)

    def local_gains():
        incoming[2].wait()
        perm = permutations()[0]
        gains = [[], []]
        for yy in range(4):
            first = pl.multiple_of(yy * 1024 + z * 256, 256)
            both = dot(GN[:, pl.ds(first, 256)], perm)
            both = jnp.where(c == 0, both[:, 0:SEG], both[:, SEG : 2 * SEG])
            for s in range(2):
                gains[s].append(both[s : s + 1])
        return [jnp.concatenate(parts, axis=1) for parts in gains]

    def first_rows():
        wait_bytes(XR.at[0:7], sx_r.at[0, 0])
        wait_bytes(RT.at[0:7], st_r.at[0])
        a, b = iota((4 * ROWS, 4 * ROWS), 0), iota((4 * ROWS, 4 * ROWS), 1)
        to_y = sum(jnp.where(a >= n * ROWS, 1, 0) for n in (1, 2, 3))
        to_t = div_by(a - to_y * ROWS, OWN)
        source = to_t * (4 * OWN) + to_y * OWN + (a - to_y * ROWS - to_t * OWN)
        arrived = dot(one_hot(b == source), XR[...].reshape(4 * ROWS, SEG))
        raw_packed = jnp.concatenate([arrived[n * ROWS : (n + 1) * ROWS] for n in range(4)], axis=1)
        raw = dot(pick(PADDED, ROWS, PAD, OWN), raw_packed.astype(BF16))
        return raw_packed, raw

    def route_column(s, k):
        return RT[...].reshape(PADDED, 128)[:, 2 * s + k : 2 * s + k + 1]

    same = iota((PAD, 128), 0) == iota((PAD, 128), 1)

    def send_squares(s, half, raw):
        squares = jnp.sum(raw * raw, axis=1, keepdims=True)
        for zz in range(4):
            part = squares[zz * PAD : (zz + 1) * PAD]
            line = jnp.sum(jnp.where(same, part, 0.0), axis=0, keepdims=True)
            SQS[s, half, zz] = jnp.broadcast_to(line, (8, 128))
        n = 1 + 2 * s + half
        send(SQS.at[s, half], SQC.at[s, half], st_s.at[n], st_r.at[n], core_peer)

    def first_product(e, activations, choice, first, count):
        gate = dot(activations, W[e, 0].reshape(LOCAL, HID))
        up = dot(activations, W[e, 1].reshape(LOCAL, HID))
        for k in range(2):
            chosen = choice[k] == float(e)
            for g, value in enumerate((gate, up)):
                value = jnp.where(chosen, value, 0.0)
                if e > 0:
                    value = PA[k, g, first : first + count] + value
                PA[k, g, first : first + count] = value

    def swap_cores(s, half):
        for k in range(2):
            for g in range(2):
                PB[s, half, k, g] = PA[k, g, half * HALF : (half + 1) * HALF].astype(BF16)
        send(PB.at[s, half, 1 - c], CR.at[s, half], sx_s.at[1 + half, s], sx_r.at[1 + half, s], core_peer)

    def sum_group(s, half):
        wait_bytes(SQC.at[s, half], st_r.at[1 + 2 * s + half])
        SQT[s, half] = SQS[s, half] + SQC[s, half]
        n = 5 + 2 * s + half
        for zz, peer in zip(z_steps, z_peers):
            send(SQT.at[s, half, zz], SQR.at[s, half, z], st_s.at[n], st_r.at[n], peer)
        SQR[s, half, z] = SQT[s, half, z]
        wait_bytes(CR.at[s, half], sx_r.at[1 + half, s])
        gate = PB[s, half, c, 0].astype(F32) + CR[s, half, 0].astype(F32)
        up = PB[s, half, c, 1].astype(F32) + CR[s, half, 1].astype(F32)
        for zz in range(4):
            cut = slice(zz * PAD, (zz + 1) * PAD)
            TB[s, half, zz] = jnp.concatenate([gate[cut], up[cut]], axis=0).astype(BF16)
        for zz, peer in zip(z_steps, z_peers):
            send(TB.at[s, half, zz], ZR.at[s, half, z], sx_s.at[3 + half, s], sx_r.at[3 + half, s], peer)
        ZR[s, half, z] = TB[s, half, z]

    def hidden_units(s, half):
        wait_bytes(SQR.at[s, half, 0:3], st_r.at[5 + 2 * s + half])
        total = jnp.sum(SQR[s, half][:, 0, :], axis=0, keepdims=True)
        scale_line = lax.rsqrt(total / float(D) + 1e-06)
        scale = jnp.sum(jnp.where(same, scale_line, 0.0), axis=1, keepdims=True)
        routes = RT[4 * half + z]
        share = jnp.where(c == 0, routes[:, 4 + 2 * s : 5 + 2 * s], routes[:, 5 + 2 * s : 6 + 2 * s])
        wait_bytes(ZR.at[s, half, 0:3], sx_r.at[3 + half, s])
        parts = [ZR[s, half, zz].astype(F32) for zz in range(4)]
        both = (parts[0] + parts[1]) + (parts[2] + parts[3])
        gate, up = both[0:PAD] * scale, both[PAD:BOTH] * scale
        units = jax.nn.silu(gate) * up * share
        blocks = [units[:, i * 128 : (i + 1) * 128] for i in range(3)]
        blocks.append(jnp.zeros((PACKED - 3 * PAD, 128), F32))
        HB[s, half, z] = jnp.concatenate(blocks, axis=0).astype(BF16)
        for peer in z_peers:
            send(HB.at[s, half, z], HB.at[s, half, z], sx_s.at[5 + half, s], sx_r.at[5 + half, s], peer)

    def swap_hidden(s, half):
        wait_bytes(HB.at[s, half, 0:3], sx_r.at[5 + half, s])
        send(HB.at[s, half], HO.at[s, half], sx_s.at[7 + half, s], sx_r.at[7 + half, s], core_peer)

    def second_product(units, choice, total):
        flat = dot(pack, units.reshape(4 * PACKED, 128))
        flat = jnp.concatenate([flat[i * HALF_ROWS : (i + 1) * HALF_ROWS] for i in range(3)], axis=1)
        for e in range(EXPERTS):
            mine = jnp.where(choice == float(e), flat, 0.0).astype(BF16)
            part = dot_last(mine, W[4 + e // 2, e % 2].reshape(LOCAL, HID))
            total = part if total is None else total + part
        return total

    def send_sums(s, half, total):
        for hh in range(4):
            YB[s, half, hh] = total[:, hh * SEG : (hh + 1) * SEG].astype(BF16)
        for peer in rep_peers:
            src = YB.at[s, half, peer[0]]
            send(src, YR.at[s, half, h], sx_s.at[9 + half, s], sx_r.at[9 + half, s], peer)
        YR[s, half, h] = YB[s, half, h]

    def branch_part(s, half):
        wait_bytes(YR.at[s, half, 0:3], sx_r.at[9 + half, s])
        parts = [YR[s, half, hh].astype(F32) for hh in range(4)]
        return ((parts[0] + parts[1]) + (parts[2] + parts[3])).astype(BF16)

    def share_part(half, part):
        BR[half, h] = part
        for peer in rep_peers:
            send(BR.at[half, h], BR.at[half, h], sx_s.at[11, half], sx_r.at[11, half], peer)

    def middle_rows(half):
        wait_bytes(BR.at[half, 0:3], sx_r.at[11, half])
        branch = jnp.concatenate([BR[half, hh] for hh in range(4)], axis=1).astype(F32)
        middle = (raw_packed[half * HALF_ROWS : (half + 1) * HALF_ROWS] + branch).astype(BF16)
        return dot(unpack, middle)

    def send_home(s, half, part):
        OB[s, 4 * half : 4 * half + 4] = dot(spread, part).astype(BF16).reshape(4, WIDE, SEG)

        @pl.when(c == half)
        def _():
            OR[s, t] = OB[s, t]
            for zz, peer in zip(z_steps, z_peers):
                send(OB.at[s, 4 * half + zz], OR.at[s, t], sx_s.at[12, s], sx_r.at[12, s], peer)

        @pl.when(c != half)
        def _():
            for zz in [z] + z_steps:
                peer = (h, at(y, zz, x, half))
                send(OB.at[s, 4 * half + zz], OR.at[s, t], sx_s.at[12, s], sx_r.at[12, s], peer)

    def store_home(s):
        wait_bytes(OR.at[s, 0:7], sx_r.at[12, s])
        perm_back = permutations()[1]
        for zz in range(4):
            both = jnp.concatenate([OR[s, zz], OR[s, 4 + zz]], axis=1)
            out[s, :, zz * 256 : (zz + 1) * 256] = dot(both, perm_back).astype(BF16)[0:OWN]

    cut_rows()
    incoming[0].wait()
    pl.semaphore_wait(barrier, len(everyone))
    send_across(0)
    send_plain(0)
    send_across(1)
    gains = local_gains()
    send_summed(0)
    send_plain(1)
    send_across(2)
    send_summed(1)
    send_plain(2)
    send_across(3)
    for copy in incoming[4:7]:
        copy.wait()
    refit(0)
    send_summed(2)
    send_plain(3)
    pass_on(0)
    refit(1)
    send_summed(3)
    send_across(4)
    send_plain(4)
    send_rows()
    send_across(5)
    send_plain(5)
    pass_on(1)
    refit(2)
    refit(3)
    pass_on(2)
    send_summed(4)
    pass_on(3)
    raw_packed, raw = first_rows()
    acts = (raw * gains[0]).astype(BF16)
    choice = [route_column(0, k) for k in range(2)]
    for half in range(2):
        send_squares(0, half, raw[half * HALF : (half + 1) * HALF])
    send_summed(5)
    for e in range(EXPERTS):
        if e == 3:
            refit(4)
        gathered(e)
        first_product(e, acts, choice, 0, PADDED)
    for half in range(2):
        swap_cores(0, half)
    pass_on(4)
    for half in range(2):
        sum_group(0, half)
    refit(5)

    a, b = iota((3 * HALF_ROWS, 4 * PACKED), 0), iota((3 * HALF_ROWS, 4 * PACKED), 1)
    to_block = jnp.where(a >= HALF_ROWS, 1, 0) + jnp.where(a >= 2 * HALF_ROWS, 1, 0)
    to_z = div_by(a - to_block * HALF_ROWS, OWN)
    row = a - to_block * HALF_ROWS - to_z * OWN
    from_z = jnp.where(b >= PACKED, 1, 0) + jnp.where(b >= 2 * PACKED, 1, 0) + jnp.where(b >= 3 * PACKED, 1, 0)
    pack = one_hot(b == from_z * PACKED + to_block * PAD + row)
    pack = jnp.where(from_z == to_z, pack, jnp.zeros_like(pack))
    unpack = pick(HALF, HALF_ROWS, PAD, OWN)
    spread = pick(4 * WIDE, HALF_ROWS, WIDE, OWN)
    ids_packed = dot(pick(ROWS, PADDED, OWN, PAD), RT[...].reshape(PADDED, 128).astype(BF16))

    def packed_choice(s, k, half):
        return ids_packed[half * HALF_ROWS : (half + 1) * HALF_ROWS, 2 * s + k : 2 * s + k + 1]

    def own_and_other(s, half):
        one, two = packed_choice(s, 0, half), packed_choice(s, 1, half)
        return jnp.where(c == 0, one, two), jnp.where(c == 0, two, one)

    def from_sums_to_parts(s):
        for half in range(2):
            hidden_units(s, half)
        if s == 0:
            gathered(4)
            gathered(5)
        for half in range(2):
            own, other = own_and_other(s, half)
            swap_hidden(s, half)
            total = second_product(HB[s, half], own, None)
            wait_bytes(HO.at[s, half], sx_r.at[7 + half, s])
            send_sums(s, half, second_product(HO[s, half], other, total))

    pass_on(5)
    from_sums_to_parts(0)
    parts = []
    for half in range(2):
        parts.append(branch_part(0, half))
        share_part(half, parts[half])
    for half in range(2):
        send_home(0, half, parts[half])
    for half in range(2):
        raw = middle_rows(half)
        acts = (raw * gains[1]).astype(BF16)
        choice = [route_column(1, k)[half * HALF : (half + 1) * HALF] for k in range(2)]
        for e in range(EXPERTS):
            first_product(e, acts, choice, half * HALF, HALF)
        swap_cores(1, half)
        send_squares(1, half, raw)
        sum_group(1, half)
    from_sums_to_parts(1)
    store_home(0)
    for half in range(2):
        send_home(1, half, branch_part(1, half))
    store_home(1)

    for b in range(BATCHES):
        for way in range(2):
            wait_bytes(RA.at[b, way], sa_s.at[b, way])
            wait_bytes(RR.at[b, way], sr_s.at[b, way])
            where = pieces(b)
            pltpu.make_async_copy((N1, N2)[way].at[where], (new1, new2)[way].at[where], out_sem.at[b, way]).wait()
        for p in range(2):
            wait_bytes(W.at[b, p, 0, 0:3], ag_s.at[b, 0, p])
            wait_bytes(W.at[b, p, 0:3], ag_s.at[b, 1, p])
    wait_bytes(XS.at[0:7], sx_s.at[0, 0])
    wait_bytes(RT.at[0:7], st_s.at[0])
    for half in range(2):
        wait_bytes(BR.at[half, 0:3], sx_s.at[11, half])
    for s in range(2):
        for half in range(2):
            wait_bytes(SQC.at[s, half], st_s.at[1 + 2 * s + half])
            wait_bytes(SQR.at[s, half, 0:3], st_s.at[5 + 2 * s + half])
            wait_bytes(CR.at[s, half], sx_s.at[1 + half, s])
            wait_bytes(ZR.at[s, half, 0:3], sx_s.at[3 + half, s])
            wait_bytes(HB.at[s, half, 0:3], sx_s.at[5 + half, s])
            wait_bytes(HO.at[s, half], sx_s.at[7 + half, s])
            wait_bytes(YR.at[s, half, 0:3], sx_s.at[9 + half, s])
        wait_bytes(OR.at[s, 0:7], sx_s.at[12, s])


def shards(grad_stack, master_weight, moment_one, moment_two, decode_rows, norm_gain, route_ids, route_weights):
    dma = pltpu.SemaphoreType.DMA
    vmem = pltpu.VMEM
    scratch = [
        vmem((EXPERTS, 3, SLICE, 4 * HID), BF16),
        vmem((3, EXPERTS, 3, SLICE, HID), F32),
        vmem((EXPERTS, 3, SLICE, HID), F32),
        vmem((EXPERTS, 3, SLICE, HID), F32),
        vmem((BATCHES, 2, 4, 4, SLICE, HID), BF16),
        vmem((BATCHES, 2, 2, 16, HID), BF16),
        vmem((BATCHES, 2, 2, 16, HID), BF16),
        vmem((BATCHES, 2, 2, SLICE, HID), BF16),
        vmem((OWN, D), BF16),
        vmem((2, D), BF16),
        vmem((2, 2, OWN), jnp.int32),
        vmem((2, 2, OWN), F32),
        vmem((WIDE, D), BF16),
        vmem((GROUP, 4 * OWN, SEG), BF16),
        vmem((GROUP, 4 * OWN, SEG), BF16),
        vmem((GROUP, PAD, 128), F32),
        vmem((2, 2, PADDED, HID), F32),
        vmem((2, 2, 2, 2, HALF, HID), BF16),
        vmem((2, 2, 2, HALF, HID), BF16),
        vmem((2, 2, 4, BOTH, HID), BF16),
        vmem((2, 2, 4, BOTH, HID), BF16),
        vmem((2, 2, 4, 8, 128), F32),
        vmem((2, 2, 4, 8, 128), F32),
        vmem((2, 2, 4, 8, 128), F32),
        vmem((2, 2, 4, 8, 128), F32),
        vmem((2, 2, 4, PACKED, 128), BF16),
        vmem((2, 2, 4, PACKED, 128), BF16),
        vmem((2, 2, 4, HALF_ROWS, SEG), BF16),
        vmem((2, 2, 4, HALF_ROWS, SEG), BF16),
        vmem((2, 4, HALF_ROWS, SEG), BF16),
        vmem((2, GROUP, WIDE, SEG), BF16),
        vmem((2, GROUP, WIDE, SEG), BF16),
        dma((8,)),
        dma((BATCHES, 2)),
        dma((BATCHES, 2)),
        dma((BATCHES, 2)),
        dma((BATCHES, 2)),
        dma((BATCHES, 2)),
        dma((BATCHES, 2, 2)),
        dma((BATCHES, 2, 2)),
        dma((13, 2)),
        dma((13, 2)),
        dma((9,)),
        dma((9,)),
    ]
    in_vmem = pl.BlockSpec(memory_space=pltpu.VMEM)
    in_hbm = pl.BlockSpec(memory_space=pltpu.HBM)
    return pl.pallas_call(
        kernel,
        out_shape=(
            jax.ShapeDtypeStruct(moment_one.shape, F32),
            jax.ShapeDtypeStruct(moment_two.shape, F32),
            jax.ShapeDtypeStruct((2, OWN, D // 4), BF16),
        ),
        in_specs=[in_hbm] * 8,
        out_specs=(in_hbm, in_hbm, in_vmem),
        scratch_shapes=scratch,
        compiler_params=pltpu.CompilerParams(
            collective_id=0, has_side_effects=True, vmem_limit_bytes=62 * 1024 * 1024
        ),
        name="refit_and_decode",
    )(
        grad_stack,
        master_weight,
        moment_one,
        moment_two,
        decode_rows,
        norm_gain,
        route_ids.transpose(0, 2, 1),
        route_weights.transpose(0, 2, 1),
    )


def solution(mesh):
    return jax.shard_map(
        shards,
        mesh=mesh,
        in_specs=(
            P("rep", None, None, "shard", None),
            P(None, None, "shard", "rep"),
            P(None, None, "shard", "rep"),
            P(None, None, "shard", "rep"),
            P("shard", None),
            P(),
            P(None, "shard", None),
            P(None, "shard", None),
        ),
        out_specs=(
            P(None, None, "shard", "rep"),
            P(None, None, "shard", "rep"),
            P(None, "shard", "rep"),
        ),
        check_vma=False,
    )
```

```python
import jax
import jax.numpy as jnp
from jax import lax
from jax.experimental import pallas as pl
from jax.experimental.pallas import tpu as pltpu
from jax.sharding import PartitionSpec as P

beta_one = 0.9
beta_two = 0.95
learn_rate = 0.05
adam_eps = 1e-08
bias_one = 1.0 - 0.9**10
bias_two = 1.0 - 0.95**10

MESH = pl.DeviceIdType.MESH
F32 = jnp.float32
BF16 = jnp.bfloat16

EXPERTS = 4
D = 4096
SLICE = 32
HID = 384
OWN = 20
PAD = 24
WIDE = 32
GROUP = 8
ROWS = OWN * GROUP
PADDED = PAD * GROUP
HALF = PADDED // 2
HALF_ROWS = ROWS // 2
BOTH = 2 * PAD
PACKED = 80
LOCAL = 512
BATCHES = 6
SEG = 128


def div_by(value, count):
    scale = {20: 3277, 24: 2731}[count]
    return (value * scale) >> 16


def iota(shape, dim):
    return lax.broadcasted_iota(jnp.int32, shape, dim)


def one_hot(mask):
    return jnp.where(mask, 1.0, 0.0).astype(BF16)


def dot(a, b):
    return jnp.dot(a, b, preferred_element_type=F32)


def dot_last(a, b):
    return lax.dot_general(a, b, (((1,), (1,)), ((), ())), preferred_element_type=F32)


def wait_bytes(ref, sem):
    pltpu.make_async_copy(ref, ref, sem).wait()


def kernel(
    grads,
    master,
    mom1,
    mom2,
    rows,
    gain,
    ids,
    weights,
    new1,
    new2,
    out,
    GV,
    MV,
    N1,
    N2,
    W,
    RA,
    SB,
    RR,
    RV,
    GN,
    IV,
    WV,
    R32,
    XS,
    XR,
    RT,
    PA,
    PB,
    CR,
    TB,
    ZR,
    SQS,
    SQC,
    SQT,
    SQR,
    HB,
    HO,
    YB,
    YR,
    BR,
    OB,
    OR,
    in_sem,
    out_sem,
    sa_s,
    sa_r,
    sr_s,
    sr_r,
    ag_s,
    ag_r,
    sx_s,
    sx_r,
    st_s,
    st_r,
):
    h = lax.axis_index("rep")
    shard = lax.axis_index("shard")
    c = lax.rem(shard, 2)
    x = lax.rem(lax.div(shard, 2), 4)
    z = lax.rem(lax.div(shard, 8), 4)
    y = lax.div(shard, 32)
    t = c * 4 + z

    def at(yy, zz, xx, cc):
        return ((yy * 4 + zz) * 4 + xx) * 2 + cc

    def ahead(value, by):
        return lax.rem(value + by, 4)

    rep_peers = [(ahead(h, by), shard) for by in (1, 2, 3)]
    x_peers = [(h, at(y, z, ahead(x, by), c)) for by in (1, 2, 3)]
    y_peers = [(h, at(ahead(y, by), z, x, c)) for by in (1, 2, 3)]
    z_steps = [ahead(z, by) for by in (1, 2, 3)]
    z_peers = [(h, at(y, zz, x, c)) for zz in z_steps]
    core_peer = (h, at(y, z, x, 1 - c))
    group_steps = [(zz, c) for zz in z_steps]
    group_steps += [(zz, 1 - c) for zz in [z] + z_steps]
    group_peers = [(h, at(y, zz, x, cc)) for zz, cc in group_steps]

    place = 4 * h + z

    def near(by, cc):
        there = lax.rem(place + by + 16, 16)
        return (lax.div(there, 4), at(y, lax.rem(there, 4), x, cc))

    two = jnp.where(lax.rem(place, 2) == 0, 2, -2)
    near_steps = [(by, cc) for by in (1, -1, two) for cc in (0, 1)]

    def send(src, dst, s_sem, r_sem, to):
        pltpu.make_async_remote_copy(
            src_ref=src,
            dst_ref=dst,
            send_sem=s_sem,
            recv_sem=r_sem,
            device_id=to,
            device_id_type=MESH,
        ).start()

    barrier = pltpu.get_barrier_semaphore()
    everyone = rep_peers + x_peers + y_peers + group_peers
    everyone += [near(by, cc) for by in (1, -1, 2, -2) for cc in (0, 1)]
    for peer in everyone:
        pl.semaphore_signal(barrier, inc=1, device_id=peer, device_id_type=MESH)
    incoming = [
        pltpu.make_async_copy(grads.at[0], GV, in_sem.at[0]),
        pltpu.make_async_copy(rows, RV, in_sem.at[1]),
        pltpu.make_async_copy(gain, GN, in_sem.at[2]),
        pltpu.make_async_copy(ids, IV, in_sem.at[3]),
        pltpu.make_async_copy(master, MV.at[0], in_sem.at[4]),
        pltpu.make_async_copy(mom1, MV.at[1], in_sem.at[5]),
        pltpu.make_async_copy(mom2, MV.at[2], in_sem.at[6]),
        pltpu.make_async_copy(weights, WV, in_sem.at[7]),
    ]
    for copy in incoming:
        copy.start()

    def pick(n_to, n_from, to_len, from_len):
        a, b = iota((n_to, n_from), 0), iota((n_to, n_from), 1)
        ta = a >> 5 if to_len == 32 else div_by(a, to_len)
        tb = b >> 5 if from_len == 32 else div_by(b, from_len)
        ia, ib = a - ta * to_len, b - tb * from_len
        return one_hot((ta == tb) & (ia == ib) & (ia < OWN))

    hp, hm, h2 = ahead(h, 1), ahead(h, 3), ahead(h, 2)
    up_peer, down_peer = (hp, shard), (hm, shard)

    def columns(owner):
        return pl.ds(pl.multiple_of(owner * HID, HID), HID)

    def pieces(b):
        if b < 4:
            return (b, slice(0, 2))
        return (slice(2 * (b - 4), 2 * (b - 4) + 2), 2)

    def grad_at(b, first, last, owner):
        return (*pieces(b), slice(first, last), columns(owner))

    def send_across(b):
        send(GV.at[grad_at(b, 0, 16, h2)], RA.at[b, 0], sa_s.at[b, 0], sa_r.at[b, 0], up_peer)
        send(GV.at[grad_at(b, 16, 32, h2)], RA.at[b, 1], sa_s.at[b, 1], sa_r.at[b, 1], down_peer)

    def send_plain(b):
        src = GV.at[grad_at(b, 16, 32, hp)]
        send(src, RR.at[b, 0, :, 16:32], sr_s.at[b, 0], sr_r.at[b, 0], up_peer)
        src = GV.at[grad_at(b, 0, 16, hm)]
        send(src, RR.at[b, 1, :, 0:16], sr_s.at[b, 1], sr_r.at[b, 1], down_peer)

    def send_summed(b):
        wait_bytes(RA.at[b, 0], sa_r.at[b, 0])
        SB[b, 0] = (RA[b, 0].astype(F32) + GV[grad_at(b, 0, 16, hp)].astype(F32)).astype(BF16)
        send(SB.at[b, 0], RR.at[b, 0, :, 0:16], sr_s.at[b, 0], sr_r.at[b, 0], up_peer)
        wait_bytes(RA.at[b, 1], sa_r.at[b, 1])
        SB[b, 1] = (RA[b, 1].astype(F32) + GV[grad_at(b, 16, 32, hm)].astype(F32)).astype(BF16)
        send(SB.at[b, 1], RR.at[b, 1, :, 16:32], sr_s.at[b, 1], sr_r.at[b, 1], down_peer)

    def refit(b):
        wait_bytes(RR.at[b, 0], sr_r.at[b, 0])
        wait_bytes(RR.at[b, 1], sr_r.at[b, 1])
        total = GV[grad_at(b, 0, 32, h)].astype(F32) + RR[b, 0].astype(F32) + RR[b, 1].astype(F32)
        mean = total * 0.25
        where = pieces(b)
        one = beta_one * MV[(1, *where)] + (1.0 - beta_one) * mean
        two = beta_two * MV[(2, *where)] + (1.0 - beta_two) * mean * mean
        update = one / bias_one / (jnp.sqrt(two / bias_two) + adam_eps)
        W[b, :, y, x] = (MV[(0, *where)] - learn_rate * update).astype(BF16)
        for peer in x_peers:
            send(W.at[b, 0, y, x], W.at[b, 0, y, x], ag_s.at[b, 0, 0], ag_r.at[b, 0, 0], peer)
        for peer in y_peers:
            send(W.at[b, 1, y, x], W.at[b, 1, y, x], ag_s.at[b, 0, 1], ag_r.at[b, 0, 1], peer)
        N1[where] = one
        N2[where] = two
        pltpu.make_async_copy(N1.at[where], new1.at[where], out_sem.at[b, 0]).start()
        pltpu.make_async_copy(N2.at[where], new2.at[where], out_sem.at[b, 1]).start()

    def pass_on(b):
        wait_bytes(W.at[b, 0, 0, 0:3], ag_r.at[b, 0, 0])
        for peer in y_peers:
            send(W.at[b, 0, y], W.at[b, 0, y], ag_s.at[b, 1, 0], ag_r.at[b, 1, 0], peer)
        wait_bytes(W.at[b, 1, 0, 0:3], ag_r.at[b, 0, 1])
        for peer in x_peers:
            send(W.at[b, 1, :, x], W.at[b, 1, :, x], ag_s.at[b, 1, 1], ag_r.at[b, 1, 1], peer)

    def gathered(b):
        wait_bytes(W.at[b, 0, 0:3], ag_r.at[b, 1, 0])
        wait_bytes(W.at[b, 1, 0:3], ag_r.at[b, 1, 1])

    def permutations():
        q = iota((256, 256), 1)
        r = iota((256, 256), 0)
        q_src = ((q & 127) >> 5) * 64 + (q >> 7) * 32 + (q & 31)
        r_src = ((r & 127) >> 5) * 64 + (r >> 7) * 32 + (r & 31)
        return one_hot(r == q_src), one_hot(q == r_src)

    def cut_rows():
        R32[...] = jnp.zeros(R32.shape, BF16)
        perm = permutations()[0]
        incoming[3].wait()
        incoming[7].wait()
        diagonal = iota((PAD, OWN), 0) == iota((PAD, OWN), 1)
        lane = iota((PAD, 128), 1)
        tile = jnp.zeros((PAD, 128), F32)
        for s in range(2):
            for k in range(2):
                for first, line in ((0, IV[s, k : k + 1].astype(F32)), (4, WV[s, k : k + 1])):
                    column = jnp.sum(jnp.where(diagonal, line, 0.0), axis=1, keepdims=True)
                    tile = jnp.where(lane == first + 2 * s + k, column, tile)
        RT[t] = tile
        incoming[1].wait()
        R32[0:OWN, :] = RV[...]
        blocks = [R32[:, (4 * yy + zz) * 256 : (4 * yy + zz + 1) * 256] for zz in range(4) for yy in range(4)]
        moved = dot(jnp.concatenate(blocks, axis=0), perm).astype(BF16)
        moved = dot(pick(16 * OWN, 16 * WIDE, OWN, WIDE), moved).astype(BF16)
        for zz in range(4):
            XS[zz] = moved[4 * zz * OWN : 4 * (zz + 1) * OWN, 0:SEG]
            XS[4 + zz] = moved[4 * zz * OWN : 4 * (zz + 1) * OWN, SEG : 2 * SEG]
        XR[t] = XS[t]

    def send_rows():
        for by, cc in near_steps:
            zz = lax.rem(place + by + 16, 4)
            send(XS.at[4 * cc + zz], XR.at[t], sx_s.at[0, 0], sx_r.at[0, 0], near(by, cc))
            send(RT.at[t], RT.at[t], st_s.at[0], st_r.at[0], near(by, cc))
        send(XS.at[4 * (1 - c) + z], XR.at[t], sx_s.at[0, 0], sx_r.at[0, 0], core_peer)
        send(RT.at[t], RT.at[t], st_s.at[0], st_r.at[0], core_peer)

    def local_gains():
        incoming[2].wait()
        perm = permutations()[0]
        gains = [[], []]
        for yy in range(4):
            first = pl.multiple_of(yy * 1024 + z * 256, 256)
            both = dot(GN[:, pl.ds(first, 256)], perm)
            both = jnp.where(c == 0, both[:, 0:SEG], both[:, SEG : 2 * SEG])
            for s in range(2):
                gains[s].append(both[s : s + 1])
        return [jnp.concatenate(parts, axis=1) for parts in gains]

    def first_rows():
        wait_bytes(XR.at[0:7], sx_r.at[0, 0])
        wait_bytes(RT.at[0:7], st_r.at[0])
        a, b = iota((4 * ROWS, 4 * ROWS), 0), iota((4 * ROWS, 4 * ROWS), 1)
        to_y = sum(jnp.where(a >= n * ROWS, 1, 0) for n in (1, 2, 3))
        to_t = div_by(a - to_y * ROWS, OWN)
        source = to_t * (4 * OWN) + to_y * OWN + (a - to_y * ROWS - to_t * OWN)
        arrived = dot(one_hot(b == source), XR[...].reshape(4 * ROWS, SEG))
        raw_packed = jnp.concatenate([arrived[n * ROWS : (n + 1) * ROWS] for n in range(4)], axis=1)
        raw = dot(pick(PADDED, ROWS, PAD, OWN), raw_packed.astype(BF16))
        return raw_packed, raw

    def route_column(s, k):
        return RT[...].reshape(PADDED, 128)[:, 2 * s + k : 2 * s + k + 1]

    same = iota((PAD, 128), 0) == iota((PAD, 128), 1)

    def send_squares(s, half, raw):
        squares = jnp.sum(raw * raw, axis=1, keepdims=True)
        for zz in range(4):
            part = squares[zz * PAD : (zz + 1) * PAD]
            line = jnp.sum(jnp.where(same, part, 0.0), axis=0, keepdims=True)
            SQS[s, half, zz] = jnp.broadcast_to(line, (8, 128))
        n = 1 + 2 * s + half
        send(SQS.at[s, half], SQC.at[s, half], st_s.at[n], st_r.at[n], core_peer)

    def first_product(e, activations, choice, first, count):
        gate = dot(activations, W[e, 0].reshape(LOCAL, HID))
        up = dot(activations, W[e, 1].reshape(LOCAL, HID))
        for k in range(2):
            chosen = choice[k] == float(e)
            for g, value in enumerate((gate, up)):
                value = jnp.where(chosen, value, 0.0)
                if e > 0:
                    value = PA[k, g, first : first + count] + value
                PA[k, g, first : first + count] = value

    def swap_cores(s, half):
        for k in range(2):
            for g in range(2):
                PB[s, half, k, g] = PA[k, g, half * HALF : (half + 1) * HALF].astype(BF16)
        send(PB.at[s, half, 1 - c], CR.at[s, half], sx_s.at[1 + half, s], sx_r.at[1 + half, s], core_peer)

    def sum_group(s, half):
        wait_bytes(SQC.at[s, half], st_r.at[1 + 2 * s + half])
        SQT[s, half] = SQS[s, half] + SQC[s, half]
        n = 5 + 2 * s + half
        for zz, peer in zip(z_steps, z_peers):
            send(SQT.at[s, half, zz], SQR.at[s, half, z], st_s.at[n], st_r.at[n], peer)
        SQR[s, half, z] = SQT[s, half, z]
        wait_bytes(CR.at[s, half], sx_r.at[1 + half, s])
        gate = PB[s, half, c, 0].astype(F32) + CR[s, half, 0].astype(F32)
        up = PB[s, half, c, 1].astype(F32) + CR[s, half, 1].astype(F32)
        for zz in range(4):
            cut = slice(zz * PAD, (zz + 1) * PAD)
            TB[s, half, zz] = jnp.concatenate([gate[cut], up[cut]], axis=0).astype(BF16)
        for zz, peer in zip(z_steps, z_peers):
            send(TB.at[s, half, zz], ZR.at[s, half, z], sx_s.at[3 + half, s], sx_r.at[3 + half, s], peer)
        ZR[s, half, z] = TB[s, half, z]

    def hidden_units(s, half):
        wait_bytes(SQR.at[s, half, 0:3], st_r.at[5 + 2 * s + half])
        total = jnp.sum(SQR[s, half][:, 0, :], axis=0, keepdims=True)
        scale_line = lax.rsqrt(total / float(D) + 1e-06)
        scale = jnp.sum(jnp.where(same, scale_line, 0.0), axis=1, keepdims=True)
        routes = RT[4 * half + z]
        share = jnp.where(c == 0, routes[:, 4 + 2 * s : 5 + 2 * s], routes[:, 5 + 2 * s : 6 + 2 * s])
        wait_bytes(ZR.at[s, half, 0:3], sx_r.at[3 + half, s])
        parts = [ZR[s, half, zz].astype(F32) for zz in range(4)]
        both = (parts[0] + parts[1]) + (parts[2] + parts[3])
        gate, up = both[0:PAD] * scale, both[PAD:BOTH] * scale
        units = jax.nn.silu(gate) * up * share
        blocks = [units[:, i * 128 : (i + 1) * 128] for i in range(3)]
        blocks.append(jnp.zeros((PACKED - 3 * PAD, 128), F32))
        HB[s, half, z] = jnp.concatenate(blocks, axis=0).astype(BF16)
        for peer in z_peers:
            send(HB.at[s, half, z], HB.at[s, half, z], sx_s.at[5 + half, s], sx_r.at[5 + half, s], peer)

    def swap_hidden(s, half):
        wait_bytes(HB.at[s, half, 0:3], sx_r.at[5 + half, s])
        send(HB.at[s, half], HO.at[s, half], sx_s.at[7 + half, s], sx_r.at[7 + half, s], core_peer)

    def second_product(units, choice, total):
        flat = dot(pack, units.reshape(4 * PACKED, 128))
        flat = jnp.concatenate([flat[i * HALF_ROWS : (i + 1) * HALF_ROWS] for i in range(3)], axis=1)
        for e in range(EXPERTS):
            mine = jnp.where(choice == float(e), flat, 0.0).astype(BF16)
            part = dot_last(mine, W[4 + e // 2, e % 2].reshape(LOCAL, HID))
            total = part if total is None else total + part
        return total

    def send_sums(s, half, total):
        for hh in range(4):
            YB[s, half, hh] = total[:, hh * SEG : (hh + 1) * SEG].astype(BF16)
        for peer in rep_peers:
            src = YB.at[s, half, peer[0]]
            send(src, YR.at[s, half, h], sx_s.at[9 + half, s], sx_r.at[9 + half, s], peer)
        YR[s, half, h] = YB[s, half, h]

    def branch_part(s, half):
        wait_bytes(YR.at[s, half, 0:3], sx_r.at[9 + half, s])
        parts = [YR[s, half, hh].astype(F32) for hh in range(4)]
        return ((parts[0] + parts[1]) + (parts[2] + parts[3])).astype(BF16)

    def share_part(half, part):
        BR[half, h] = part
        for peer in rep_peers:
            send(BR.at[half, h], BR.at[half, h], sx_s.at[11, half], sx_r.at[11, half], peer)

    def middle_rows(half):
        wait_bytes(BR.at[half, 0:3], sx_r.at[11, half])
        branch = jnp.concatenate([BR[half, hh] for hh in range(4)], axis=1).astype(F32)
        middle = (raw_packed[half * HALF_ROWS : (half + 1) * HALF_ROWS] + branch).astype(BF16)
        return dot(unpack, middle)

    def send_home(s, half, part):
        OB[s, 4 * half : 4 * half + 4] = dot(spread, part).astype(BF16).reshape(4, WIDE, SEG)

        @pl.when(c == half)
        def _():
            OR[s, t] = OB[s, t]
            for zz, peer in zip(z_steps, z_peers):
                send(OB.at[s, 4 * half + zz], OR.at[s, t], sx_s.at[12, s], sx_r.at[12, s], peer)

        @pl.when(c != half)
        def _():
            for zz in [z] + z_steps:
                peer = (h, at(y, zz, x, half))
                send(OB.at[s, 4 * half + zz], OR.at[s, t], sx_s.at[12, s], sx_r.at[12, s], peer)

    def store_home(s):
        wait_bytes(OR.at[s, 0:7], sx_r.at[12, s])
        perm_back = permutations()[1]
        for zz in range(4):
            both = jnp.concatenate([OR[s, zz], OR[s, 4 + zz]], axis=1)
            out[s, :, zz * 256 : (zz + 1) * 256] = dot(both, perm_back).astype(BF16)[0:OWN]

    cut_rows()
    incoming[0].wait()
    pl.semaphore_wait(barrier, len(everyone))
    send_across(0)
    send_plain(0)
    send_across(1)
    gains = local_gains()
    send_summed(0)
    send_plain(1)
    send_across(2)
    send_summed(1)
    send_plain(2)
    send_across(3)
    for copy in incoming[4:7]:
        copy.wait()
    refit(0)
    send_summed(2)
    send_plain(3)
    pass_on(0)
    refit(1)
    send_summed(3)
    send_across(4)
    send_plain(4)
    send_rows()
    send_across(5)
    send_plain(5)
    pass_on(1)
    refit(2)
    refit(3)
    pass_on(2)
    send_summed(4)
    pass_on(3)
    raw_packed, raw = first_rows()
    acts = (raw * gains[0]).astype(BF16)
    choice = [route_column(0, k) for k in range(2)]
    for half in range(2):
        send_squares(0, half, raw[half * HALF : (half + 1) * HALF])
    send_summed(5)
    for e in range(EXPERTS):
        if e == 3:
            refit(4)
        gathered(e)
        first_product(e, acts, choice, 0, PADDED)
    for half in range(2):
        swap_cores(0, half)
    for half in range(2):
        sum_group(0, half)
    pass_on(4)
    refit(5)

    a, b = iota((3 * HALF_ROWS, 4 * PACKED), 0), iota((3 * HALF_ROWS, 4 * PACKED), 1)
    to_block = jnp.where(a >= HALF_ROWS, 1, 0) + jnp.where(a >= 2 * HALF_ROWS, 1, 0)
    to_z = div_by(a - to_block * HALF_ROWS, OWN)
    row = a - to_block * HALF_ROWS - to_z * OWN
    from_z = jnp.where(b >= PACKED, 1, 0) + jnp.where(b >= 2 * PACKED, 1, 0) + jnp.where(b >= 3 * PACKED, 1, 0)
    pack = one_hot(b == from_z * PACKED + to_block * PAD + row)
    pack = jnp.where(from_z == to_z, pack, jnp.zeros_like(pack))
    unpack = pick(HALF, HALF_ROWS, PAD, OWN)
    spread = pick(4 * WIDE, HALF_ROWS, WIDE, OWN)
    ids_packed = dot(pick(ROWS, PADDED, OWN, PAD), RT[...].reshape(PADDED, 128).astype(BF16))

    def packed_choice(s, k, half):
        return ids_packed[half * HALF_ROWS : (half + 1) * HALF_ROWS, 2 * s + k : 2 * s + k + 1]

    def own_and_other(s, half):
        one, two = packed_choice(s, 0, half), packed_choice(s, 1, half)
        return jnp.where(c == 0, one, two), jnp.where(c == 0, two, one)

    def from_sums_to_parts(s):
        for half in range(2):
            hidden_units(s, half)
        if s == 0:
            gathered(4)
            gathered(5)
        for half in range(2):
            own, other = own_and_other(s, half)
            swap_hidden(s, half)
            total = second_product(HB[s, half], own, None)
            wait_bytes(HO.at[s, half], sx_r.at[7 + half, s])
            send_sums(s, half, second_product(HO[s, half], other, total))

    pass_on(5)
    from_sums_to_parts(0)
    parts = []
    for half in range(2):
        parts.append(branch_part(0, half))
        share_part(half, parts[half])
    for half in range(2):
        send_home(0, half, parts[half])
    for half in range(2):
        raw = middle_rows(half)
        acts = (raw * gains[1]).astype(BF16)
        choice = [route_column(1, k)[half * HALF : (half + 1) * HALF] for k in range(2)]
        for e in range(EXPERTS):
            first_product(e, acts, choice, half * HALF, HALF)
        swap_cores(1, half)
        send_squares(1, half, raw)
        sum_group(1, half)
    from_sums_to_parts(1)
    store_home(0)
    for half in range(2):
        send_home(1, half, branch_part(1, half))
    store_home(1)

    for b in range(BATCHES):
        for way in range(2):
            wait_bytes(RA.at[b, way], sa_s.at[b, way])
            wait_bytes(RR.at[b, way], sr_s.at[b, way])
            where = pieces(b)
            pltpu.make_async_copy((N1, N2)[way].at[where], (new1, new2)[way].at[where], out_sem.at[b, way]).wait()
        for p in range(2):
            wait_bytes(W.at[b, p, 0, 0:3], ag_s.at[b, 0, p])
            wait_bytes(W.at[b, p, 0:3], ag_s.at[b, 1, p])
    wait_bytes(XS.at[0:7], sx_s.at[0, 0])
    wait_bytes(RT.at[0:7], st_s.at[0])
    for half in range(2):
        wait_bytes(BR.at[half, 0:3], sx_s.at[11, half])
    for s in range(2):
        for half in range(2):
            wait_bytes(SQC.at[s, half], st_s.at[1 + 2 * s + half])
            wait_bytes(SQR.at[s, half, 0:3], st_s.at[5 + 2 * s + half])
            wait_bytes(CR.at[s, half], sx_s.at[1 + half, s])
            wait_bytes(ZR.at[s, half, 0:3], sx_s.at[3 + half, s])
            wait_bytes(HB.at[s, half, 0:3], sx_s.at[5 + half, s])
            wait_bytes(HO.at[s, half], sx_s.at[7 + half, s])
            wait_bytes(YR.at[s, half, 0:3], sx_s.at[9 + half, s])
        wait_bytes(OR.at[s, 0:7], sx_s.at[12, s])


def shards(grad_stack, master_weight, moment_one, moment_two, decode_rows, norm_gain, route_ids, route_weights):
    dma = pltpu.SemaphoreType.DMA
    vmem = pltpu.VMEM
    scratch = [
        vmem((EXPERTS, 3, SLICE, 4 * HID), BF16),
        vmem((3, EXPERTS, 3, SLICE, HID), F32),
        vmem((EXPERTS, 3, SLICE, HID), F32),
        vmem((EXPERTS, 3, SLICE, HID), F32),
        vmem((BATCHES, 2, 4, 4, SLICE, HID), BF16),
        vmem((BATCHES, 2, 2, 16, HID), BF16),
        vmem((BATCHES, 2, 2, 16, HID), BF16),
        vmem((BATCHES, 2, 2, SLICE, HID), BF16),
        vmem((OWN, D), BF16),
        vmem((2, D), BF16),
        vmem((2, 2, OWN), jnp.int32),
        vmem((2, 2, OWN), F32),
        vmem((WIDE, D), BF16),
        vmem((GROUP, 4 * OWN, SEG), BF16),
        vmem((GROUP, 4 * OWN, SEG), BF16),
        vmem((GROUP, PAD, 128), F32),
        vmem((2, 2, PADDED, HID), F32),
        vmem((2, 2, 2, 2, HALF, HID), BF16),
        vmem((2, 2, 2, HALF, HID), BF16),
        vmem((2, 2, 4, BOTH, HID), BF16),
        vmem((2, 2, 4, BOTH, HID), BF16),
        vmem((2, 2, 4, 8, 128), F32),
        vmem((2, 2, 4, 8, 128), F32),
        vmem((2, 2, 4, 8, 128), F32),
        vmem((2, 2, 4, 8, 128), F32),
        vmem((2, 2, 4, PACKED, 128), BF16),
        vmem((2, 2, 4, PACKED, 128), BF16),
        vmem((2, 2, 4, HALF_ROWS, SEG), BF16),
        vmem((2, 2, 4, HALF_ROWS, SEG), BF16),
        vmem((2, 4, HALF_ROWS, SEG), BF16),
        vmem((2, GROUP, WIDE, SEG), BF16),
        vmem((2, GROUP, WIDE, SEG), BF16),
        dma((8,)),
        dma((BATCHES, 2)),
        dma((BATCHES, 2)),
        dma((BATCHES, 2)),
        dma((BATCHES, 2)),
        dma((BATCHES, 2)),
        dma((BATCHES, 2, 2)),
        dma((BATCHES, 2, 2)),
        dma((13, 2)),
        dma((13, 2)),
        dma((9,)),
        dma((9,)),
    ]
    in_vmem = pl.BlockSpec(memory_space=pltpu.VMEM)
    in_hbm = pl.BlockSpec(memory_space=pltpu.HBM)
    return pl.pallas_call(
        kernel,
        out_shape=(
            jax.ShapeDtypeStruct(moment_one.shape, F32),
            jax.ShapeDtypeStruct(moment_two.shape, F32),
            jax.ShapeDtypeStruct((2, OWN, D // 4), BF16),
        ),
        in_specs=[in_hbm] * 8,
        out_specs=(in_hbm, in_hbm, in_vmem),
        scratch_shapes=scratch,
        compiler_params=pltpu.CompilerParams(
            collective_id=0, has_side_effects=True, vmem_limit_bytes=62 * 1024 * 1024
        ),
        name="refit_and_decode",
    )(
        grad_stack,
        master_weight,
        moment_one,
        moment_two,
        decode_rows,
        norm_gain,
        route_ids.transpose(0, 2, 1),
        route_weights.transpose(0, 2, 1),
    )


def solution(mesh):
    return jax.shard_map(
        shards,
        mesh=mesh,
        in_specs=(
            P("rep", None, None, "shard", None),
            P(None, None, "shard", "rep"),
            P(None, None, "shard", "rep"),
            P(None, None, "shard", "rep"),
            P("shard", None),
            P(),
            P(None, "shard", None),
            P(None, "shard", None),
        ),
        out_specs=(
            P(None, None, "shard", "rep"),
            P(None, None, "shard", "rep"),
            P(None, "shard", "rep"),
        ),
        check_vma=False,
    )
```
